512 devices in a mesh: ta: 16 (over y, core), sa: 32 (over x, z).
Axes of the slice: x: 4, y: 8, z: 8, core: 2. Of those that a mesh axis runs over, the one named last changes fastest.
Arguments:
- gauge_links: float32 [4, 2, 3, 3, 32, 128, 128], P(None, None, None, None, 'sa', 'ta'), as said below
- noise_field: float32 [4, 8, 32, 128, 128], P(None, None, 'sa', 'ta'), may hold values from -6 to 6
Outputs:
- cooled_links: float32 [4, 2, 3, 3, 32, 128, 128], P(None, None, None, None, 'sa', 'ta')
- unitarity_norms: float32 [3, 128], P(None, 'ta')
The draws below stay inside these ranges and needn't reach their ends.
Inputs may be any that keep to these rules, and one draw needn't show every extreme that they name: `gauge_links`: every link matrix has determinant one.
All inputs are finite; a program needn't handle non-finite values.
Results may differ from the reference program's by a relative error of at most 0.0003.
Values sent between devices are 32-bit elements; how exact they have to be, the bound alone decides.
A program may use at most 192 MiB of HBM per device.

```python
import math
import jax
import jax.numpy as jnp
import numpy as np
from jax import lax

NY = 8
NZ = 16
NT = 128
NX = 32


def grid_product(former, latter):
    result = []
    for row_pos in range(3):
        row_entries = []
        for col_pos in range(3):
            real_sum = 0.0
            imag_sum = 0.0
            for inner_pos in range(3):
                real_sum = real_sum + former[row_pos][inner_pos][0] * latter[inner_pos][col_pos][0] - former[row_pos][inner_pos][1] * latter[inner_pos][col_pos][1]
                imag_sum = imag_sum + former[row_pos][inner_pos][0] * latter[inner_pos][col_pos][1] + former[row_pos][inner_pos][1] * latter[inner_pos][col_pos][0]
            row_entries.append((real_sum, imag_sum))
        result.append(row_entries)
    return result


def identity_entries(zeros):
    return [[(zeros + 1.0 if row_pos == col_pos else zeros, zeros) for col_pos in range(3)] for row_pos in range(3)]


def rotation(zeros, first_row, second_row, rotation_angle, phase_angle):
    entries = identity_entries(zeros)
    cosine = jnp.cos(rotation_angle)
    sine_value = jnp.sin(rotation_angle)
    entries[first_row][first_row] = (cosine, zeros)
    entries[second_row][second_row] = (cosine, zeros)
    entries[first_row][second_row] = (-jnp.cos(phase_angle) * sine_value, jnp.sin(phase_angle) * sine_value)
    entries[second_row][first_row] = (jnp.cos(phase_angle) * sine_value, jnp.sin(phase_angle) * sine_value)
    return entries


def draw_gauge_links(key, part):
    key = jax.random.fold_in(key, 17)
    subkeys = jax.random.split(key, 5)
    batch_shape = (4, NX, NT, NY * NZ)
    zeros = jnp.zeros(batch_shape, jnp.float32)
    angles = jax.random.uniform(subkeys[0], (3,) + batch_shape, jnp.float32, -math.pi, math.pi)
    phases = jax.random.uniform(subkeys[1], (5,) + batch_shape, jnp.float32, -math.pi, math.pi)
    position = (jnp.arange(NX, dtype=jnp.float32) / NX).reshape(1, NX, 1, 1)
    direction_scale = jnp.array([1.0, 1.0, 1.0, 0.1], jnp.float32).reshape(4, 1, 1, 1)
    spread = jnp.exp(jax.random.uniform(subkeys[2], batch_shape, jnp.float32, math.log(0.02), math.log(0.2))) * (0.5 + position)
    spread = spread * direction_scale
    stretch = 0.2 * spread * jax.random.uniform(subkeys[3], (2,) + batch_shape, jnp.float32, -1.0, 1.0)
    upper = spread * jax.random.normal(subkeys[4], (6,) + batch_shape, jnp.float32)
    diagonal = identity_entries(zeros)
    diagonal[0][0] = (jnp.exp(stretch[0]) * jnp.cos(phases[3]), jnp.exp(stretch[0]) * jnp.sin(phases[3]))
    diagonal[1][1] = (jnp.exp(stretch[1]) * jnp.cos(phases[4]), jnp.exp(stretch[1]) * jnp.sin(phases[4]))
    last_phase = -phases[3] - phases[4]
    last_stretch = jnp.exp(-stretch[0] - stretch[1])
    diagonal[2][2] = (last_stretch * jnp.cos(last_phase), last_stretch * jnp.sin(last_phase))
    nilpotent = identity_entries(zeros)
    nilpotent[0][1] = (upper[0], upper[1])
    nilpotent[0][2] = (upper[2], upper[3])
    nilpotent[1][2] = (upper[4], upper[5])
    link_grid = grid_product(rotation(zeros, 0, 1, angles[0], phases[0]), rotation(zeros, 1, 2, angles[1], phases[1]))
    link_grid = grid_product(link_grid, rotation(zeros, 0, 2, angles[2], phases[2]))
    link_grid = grid_product(link_grid, diagonal)
    link_grid = grid_product(link_grid, nilpotent)
    real_part = jnp.stack([jnp.stack([link_grid[row_pos][col_pos][0] for col_pos in range(3)]) for row_pos in range(3)])
    imag_part = jnp.stack([jnp.stack([link_grid[row_pos][col_pos][1] for col_pos in range(3)]) for row_pos in range(3)])
    return jnp.moveaxis(jnp.stack([real_part, imag_part]), 3, 0)


def shard_levels(key, extent, cuts, low, largest):
    gain, own = 1.0, jax.random.fold_in(key, 6)
    for dim, shards_of in cuts:
        draws = jnp.exp(jax.random.uniform(jax.random.fold_in(own, dim), (shards_of,), jnp.float32, low / len(cuts), largest / len(cuts)))
        gain = gain * jnp.repeat(draws, extent[dim] // shards_of).reshape([-1 if axis == dim else 1 for axis in range(len(extent))])
    return gain


def scatter_about(own_key, extent, deviation, reach, pieces=(), kind=jnp.bfloat16):
    values = deviation * jax.random.normal(own_key, extent, jnp.float32)
    if pieces:
        values = values * shard_levels(own_key, extent, pieces, -0.22, 0.18)
    return jnp.clip(values, -reach, reach).astype(kind)


def setup_inputs(seed: int = 0) -> dict:
    key_of = jax.random.split(jax.random.key(seed), 3)
    return {
        "gauge_links": draw_gauge_links(jax.random.fold_in(key_of[2], 71), 0),
        "noise_field": scatter_about(key_of[1], (4, 8, NX, NT, NY * NZ), 1.4142, 6.0, ((2, 32), (3, 16)), jnp.float32),
    }


COUPLING = 5.6
STEP_SIZE = 0.02
COOL_SIZE = 0.02
FUGACITY = 0.5
ANTI_FUGACITY = 0.02

def gell_mann():
    real_table = np.zeros((8, 3, 3), np.float32)
    imag_table = np.zeros((8, 3, 3), np.float32)
    real_table[0, 0, 1] = 1.0
    real_table[0, 1, 0] = 1.0
    imag_table[1, 0, 1] = -1.0
    imag_table[1, 1, 0] = 1.0
    real_table[2, 0, 0] = 1.0
    real_table[2, 1, 1] = -1.0
    real_table[3, 0, 2] = 1.0
    real_table[3, 2, 0] = 1.0
    imag_table[4, 0, 2] = -1.0
    imag_table[4, 2, 0] = 1.0
    real_table[5, 1, 2] = 1.0
    real_table[5, 2, 1] = 1.0
    imag_table[6, 1, 2] = -1.0
    imag_table[6, 2, 1] = 1.0
    root_three = math.sqrt(3.0)
    real_table[7, 0, 0] = 1.0 / root_three
    real_table[7, 1, 1] = 1.0 / root_three
    real_table[7, 2, 2] = -2.0 / root_three
    return (real_table, imag_table)

def elem_product(former, latter):
    return (former[0] * latter[0] - former[1] * latter[1], former[0] * latter[1] + former[1] * latter[0])

def real_matmul(former, latter):
    return lax.optimization_barrier(jnp.sum(former[:, :, None] * latter[None, :, :], axis=1))

def matrix_product(former, latter):
    return (real_matmul(former[0], latter[0]) - real_matmul(former[1], latter[1]), real_matmul(former[0], latter[1]) + real_matmul(former[1], latter[0]))

def matrix_sum(former, latter, factor):
    return (former[0] + factor * latter[0], former[1] + factor * latter[1])

def scaled(matrix, factor):
    return (factor * matrix[0], factor * matrix[1])

def dagger(matrix):
    return (jnp.swapaxes(matrix[0], 0, 1), -jnp.swapaxes(matrix[1], 0, 1))

def unit_like(matrix):
    unit_matrix = jnp.eye(3, dtype=matrix[0].dtype).reshape((3, 3) + (1,) * (matrix[0].ndim - 2))
    return (jnp.broadcast_to(unit_matrix, matrix[0].shape), jnp.zeros_like(matrix[0]))

def traceless(matrix):
    unit_real = unit_like(matrix)[0]
    trace_real = (matrix[0][0, 0] + matrix[0][1, 1] + matrix[0][2, 2]) / 3.0
    trace_imag = (matrix[1][0, 0] + matrix[1][1, 1] + matrix[1][2, 2]) / 3.0
    return (matrix[0] - unit_real * trace_real, matrix[1] - unit_real * trace_imag)

def adjugate(matrix):

    def entry(row_pos, col_pos):
        return (matrix[0][row_pos % 3, col_pos % 3], matrix[1][row_pos % 3, col_pos % 3])
    real_rows = []
    imag_rows = []
    for row_pos in range(3):
        real_entries = []
        imag_entries = []
        for col_pos in range(3):
            plus_term = elem_product(entry(col_pos + 1, row_pos + 1), entry(col_pos + 2, row_pos + 2))
            minus_term = elem_product(entry(col_pos + 1, row_pos + 2), entry(col_pos + 2, row_pos + 1))
            real_entries.append(plus_term[0] - minus_term[0])
            imag_entries.append(plus_term[1] - minus_term[1])
        real_rows.append(jnp.stack(real_entries))
        imag_rows.append(jnp.stack(imag_entries))
    return (jnp.stack(real_rows), jnp.stack(imag_rows))

def determinant(matrix, adjoint):
    result = elem_product((matrix[0][0, 0], matrix[1][0, 0]), (adjoint[0][0, 0], adjoint[1][0, 0]))
    for col_pos in (1, 2):
        addend = elem_product((matrix[0][0, col_pos], matrix[1][0, col_pos]), (adjoint[0][col_pos, 0], adjoint[1][col_pos, 0]))
        result = (result[0] + addend[0], result[1] + addend[1])
    return result

def general_inverse(matrix):
    adjoint = adjugate(matrix)
    det_value = determinant(matrix, adjoint)
    modulus = det_value[0] * det_value[0] + det_value[1] * det_value[1]
    factor = (det_value[0] / modulus, -det_value[1] / modulus)
    return elem_product(adjoint, factor)

def exp_cubic(matrix):
    square = matrix_product(matrix, matrix)
    third_power = matrix_product(square, matrix)
    result = matrix_sum(unit_like(matrix), matrix, 1.0)
    result = matrix_sum(result, square, 0.5)
    return matrix_sum(result, third_power, 1.0 / 6.0)

def noise_matrix(weights):
    real_table, imag_table = gell_mann()
    return (jnp.einsum('aij,a...->ij...', real_table, weights, precision=lax.Precision.HIGHEST), jnp.einsum('aij,a...->ij...', imag_table, weights, precision=lax.Precision.HIGHEST))

def fermion_drift(polyakov):
    unit_matrix = unit_like(polyakov)
    forward_part = scaled(polyakov, FUGACITY)
    backward_part = scaled(adjugate(polyakov), ANTI_FUGACITY)
    former = matrix_product(forward_part, general_inverse(matrix_sum(unit_matrix, forward_part, 1.0)))
    latter = matrix_product(backward_part, general_inverse(matrix_sum(unit_matrix, backward_part, 1.0)))
    return traceless(matrix_sum(former, latter, -1.0))

def unit_step(direction, orient):
    return tuple((orient if position == direction else 0 for position in range(4)))

def joined(former, latter):
    return tuple((former[position] + latter[position] for position in range(4)))

def gauge_drift(lookup, direction):
    zero_step = (0, 0, 0, 0)
    up_mu = unit_step(direction, 1)
    forward_sum = None
    backward_sum = None
    for transverse in range(4):
        if transverse == direction:
            continue
        up_nu = unit_step(transverse, 1)
        down_nu = unit_step(transverse, -1)
        corner = joined(up_mu, down_nu)
        upper_staple = matrix_product(matrix_product(lookup(0, transverse, up_mu), lookup(1, direction, up_nu)), lookup(1, transverse, zero_step))
        lower_staple = matrix_product(matrix_product(lookup(1, transverse, corner), lookup(1, direction, down_nu)), lookup(0, transverse, down_nu))
        upper_reverse = matrix_product(matrix_product(lookup(0, transverse, zero_step), lookup(0, direction, up_nu)), lookup(1, transverse, up_mu))
        lower_reverse = matrix_product(matrix_product(lookup(1, transverse, down_nu), lookup(0, direction, down_nu)), lookup(0, transverse, corner))
        forward_term = matrix_sum(upper_staple, lower_staple, 1.0)
        backward_term = matrix_sum(upper_reverse, lower_reverse, 1.0)
        forward_sum = forward_term if forward_sum is None else matrix_sum(forward_sum, forward_term, 1.0)
        backward_sum = backward_term if backward_sum is None else matrix_sum(backward_sum, backward_term, 1.0)
    plaquettes = matrix_sum(matrix_product(lookup(0, direction, zero_step), forward_sum), matrix_product(backward_sum, lookup(1, direction, zero_step)), -1.0)
    return traceless(plaquettes)

def time_slice(matrix, time_pos):
    return (matrix[0][:, :, :, time_pos], matrix[1][:, :, :, time_pos])

def stack_time(matrices):
    return (jnp.stack([matrix[0] for matrix in matrices], axis=3), jnp.stack([matrix[1] for matrix in matrices], axis=3))

def neighbor(member, offsets):
    full_shape = member.shape
    shifted = jnp.roll(member, -offsets[3], axis=member.ndim - 2)
    shifted = jnp.roll(shifted, -offsets[0], axis=member.ndim - 3)
    shifted = shifted.reshape(full_shape[:-1] + (NY, NZ))
    shifted = jnp.roll(shifted, (-offsets[1], -offsets[2]), axis=(shifted.ndim - 2, shifted.ndim - 1))
    return shifted.reshape(full_shape)

def neighbor_matrix(matrix, offsets):
    return (neighbor(matrix[0], offsets), neighbor(matrix[1], offsets))

def slice_norms(matrices):
    squares = None
    for matrix in matrices:
        addend = lax.optimization_barrier(jnp.sum(matrix[0] * matrix[0] + matrix[1] * matrix[1], axis=(0, 1)))
        squares = addend if squares is None else squares + addend
    return lax.optimization_barrier(jnp.mean(squares, axis=(0, 2))) / 4.0 - 3.0

def cool_step(matrices):
    gradient = None
    for direction in range(4):
        outer_product = matrix_product(matrices[direction], dagger(matrices[direction]))
        inner_product = matrix_product(dagger(matrices[direction]), matrices[direction])
        lagged = neighbor_matrix(inner_product, unit_step(direction, -1))
        contribution = matrix_sum(outer_product, lagged, -1.0)
        gradient = contribution if gradient is None else matrix_sum(gradient, contribution, 1.0)
    gradient = traceless(gradient)
    transform = exp_cubic(scaled(gradient, -COOL_SIZE))
    inverse_transform = exp_cubic(scaled(gradient, COOL_SIZE))
    result = []
    for direction in range(4):
        forward_inverse = neighbor_matrix(inverse_transform, unit_step(direction, 1))
        result.append(matrix_product(matrix_product(transform, matrices[direction]), forward_inverse))
    return result

def reference(gauge_links, noise_field):
    matrices = [(gauge_links[direction, 0], gauge_links[direction, 1]) for direction in range(4)]
    inverses = [adjugate(matrix) for matrix in matrices]
    tables = (matrices, inverses)

    def lookup(kind_pos, direction, offsets):
        return neighbor_matrix(tables[kind_pos][direction], offsets)
    temporal = matrices[3]
    slab_count = temporal[0].shape[3]
    prefixes = [unit_like(time_slice(temporal, 0))]
    for time_pos in range(slab_count - 1):
        prefixes.append(matrix_product(prefixes[-1], time_slice(temporal, time_pos)))
    suffixes = [time_slice(temporal, slab_count - 1)]
    for time_pos in range(slab_count - 2, -1, -1):
        suffixes.insert(0, matrix_product(time_slice(temporal, time_pos), suffixes[0]))
    drifts = [fermion_drift(matrix_product(suffixes[time_pos], prefixes[time_pos])) for time_pos in range(slab_count)]
    fermion_field = stack_time(drifts)
    updated = []
    for direction in range(4):
        exponent = scaled(gauge_drift(lookup, direction), -STEP_SIZE * COUPLING / 3.0)
        if direction == 3:
            exponent = matrix_sum(exponent, fermion_field, -4.0 * STEP_SIZE)
        random_part = noise_matrix(noise_field[direction])
        exponent = matrix_sum(exponent, (-random_part[1], random_part[0]), math.sqrt(STEP_SIZE))
        updated.append(matrix_product(exp_cubic(exponent), matrices[direction]))
    norm_rows = [slice_norms(updated)]
    current = cool_step(updated)
    norm_rows.append(slice_norms(current))
    current = cool_step(current)
    norm_rows.append(slice_norms(current))
    cooled_links = jnp.stack([jnp.stack(matrix) for matrix in current])
    return (cooled_links, jnp.stack(norm_rows))
```

```python
import functools
import math

import jax
import jax.numpy as jnp
from jax import lax
from jax.experimental import pallas as pl
from jax.experimental.pallas import tpu as pltpu
from jax.sharding import PartitionSpec as P

NY = 8
NZ = 16
LANES = NY * NZ
ROWS = 8

COUPLING = 5.6
STEP_SIZE = 0.02
COOL_SIZE = 0.02
FUGACITY = 0.5
ANTI_FUGACITY = 0.02

MESH = pl.DeviceIdType.MESH
TILE = (ROWS, LANES)
MAT = (2, 3, 3) + TILE
HERM = (9,) + TILE


def load(ref):
    return (ref[0], ref[1])


def store(ref, m):
    ref[0] = m[0]
    ref[1] = m[1]


def add(a, b):
    return (a[0] + b[0], a[1] + b[1])


def sub(a, b):
    return (a[0] - b[0], a[1] - b[1])


def mm(a, b):
    ar, ai = a
    br, bi = b
    re = im = None
    for k in range(3):
        cr, ci = ar[:, k : k + 1], ai[:, k : k + 1]
        rr, ri = br[k : k + 1], bi[k : k + 1]
        tr = cr * rr - ci * ri
        ti = cr * ri + ci * rr
        re = tr if re is None else re + tr
        im = ti if im is None else im + ti
    return (re, im)


def roll_rows(x, n):
    return jnp.concatenate([x[n:], x[:n]], axis=0)


def roll_cols(x, n):
    return jnp.concatenate([x[:, n:], x[:, :n]], axis=1)


def transposed(x):
    return jnp.stack([x[:, i] for i in range(3)])


def cmul(a, b):
    return (a[0] * b[0] - a[1] * b[1], a[0] * b[1] + a[1] * b[0])


def adj(m):
    one = tuple(roll_rows(x, 1) for x in m)
    two = tuple(roll_rows(x, 2) for x in m)
    plus = cmul(tuple(roll_cols(x, 1) for x in one), tuple(roll_cols(x, 2) for x in two))
    minus = cmul(tuple(roll_cols(x, 2) for x in one), tuple(roll_cols(x, 1) for x in two))
    return (transposed(plus[0] - minus[0]), transposed(plus[1] - minus[1]))


def less_inverse(p):
    return sub(p, adj(p))


def entry(m, i, j):
    return (m[0][i, j], m[1][i, j])


def add_diagonal(x, value):
    rows = []
    for i in range(3):
        parts = [(x[i, i] + value)[None]]
        if i > 0:
            parts.insert(0, x[i, :i])
        if i < 2:
            parts.append(x[i, i + 1 :])
        rows.append(jnp.concatenate(parts, axis=0))
    return jnp.stack(rows)


def inverse(m):
    a = adj(m)
    det = cmul(entry(m, 0, 0), entry(a, 0, 0))
    for j in (1, 2):
        det = add(det, cmul(entry(m, 0, j), entry(a, j, 0)))
    scale = 1.0 / (det[0] * det[0] + det[1] * det[1])
    factor = ((det[0] * scale)[None, None], (-det[1] * scale)[None, None])
    return cmul(a, factor)


def exp_times(y, u):
    square = mm(y, y)
    trace = tuple(x[0, 0] + x[1, 1] + x[2, 2] for x in square)
    det = None
    for j in range(3):
        a, b = (j + 1) % 3, (j + 2) % 3
        minor = sub(
            cmul(entry(y, 1, a), entry(y, 2, b)), cmul(entry(y, 1, b), entry(y, 2, a))
        )
        term = cmul(entry(y, 0, j), minor)
        det = term if det is None else add(det, term)
    beta = ((1.0 + trace[0] * (1.0 / 12.0))[None, None], (trace[1] * (1.0 / 12.0))[None, None])
    linear = cmul(y, beta)
    re = add_diagonal(linear[0] + 0.5 * square[0], 1.0 + det[0] * (1.0 / 6.0))
    im = add_diagonal(linear[1] + 0.5 * square[1], det[1] * (1.0 / 6.0))
    return mm((re, im), u)


def gram_rows(m):
    re, im = m
    diag = re * re + im * im
    a = tuple(jnp.concatenate([x[0:1], x[0:1], x[1:2]], axis=0) for x in m)
    b = tuple(jnp.concatenate([x[1:2], x[2:3], x[2:3]], axis=0) for x in m)
    pr = a[0] * b[0] + a[1] * b[1]
    pi = a[1] * b[0] - a[0] * b[1]
    return tuple(x[:, 0] + x[:, 1] + x[:, 2] for x in (diag, pr, pi))


def gram_cols(m):
    re, im = m
    diag = re * re + im * im
    a = tuple(jnp.concatenate([x[:, 0:1], x[:, 0:1], x[:, 1:2]], axis=1) for x in m)
    b = tuple(jnp.concatenate([x[:, 1:2], x[:, 2:3], x[:, 2:3]], axis=1) for x in m)
    pr = a[0] * b[0] + a[1] * b[1]
    pi = a[0] * b[1] - a[1] * b[0]
    return tuple(x[0] + x[1] + x[2] for x in (diag, pr, pi))


def h_add(a, b):
    return tuple(x + y for x, y in zip(a, b))


def h_sub(a, b):
    return tuple(x - y for x, y in zip(a, b))


def h_pack(h):
    return jnp.concatenate(h, axis=0)


def h_unpack(x):
    return (x[0:3], x[3:6], x[6:9])


def h_offsets(h):
    _, r, i = h
    one = (jnp.stack([r[0], r[2], r[1]]), jnp.stack([i[0], i[2], -i[1]]))
    two = (jnp.stack([r[1], r[0], r[2]]), jnp.stack([i[1], -i[0], -i[2]]))
    return one, two


def h_times(h, m):
    d = h[0][:, None]
    one, two = h_offsets(h)
    re, im = d * m[0], d * m[1]
    for n, off in ((1, one), (2, two)):
        r, i = off[0][:, None], off[1][:, None]
        ur, ui = roll_rows(m[0], n), roll_rows(m[1], n)
        re = re + r * ur - i * ui
        im = im + r * ui + i * ur
    return (re, im)


def times_h(m, h):
    d = h[0][None]
    one, two = h_offsets(h)
    re, im = m[0] * d, m[1] * d
    for n, off in ((1, one), (2, two)):
        r, i = off[0][None], off[1][None]
        ur, ui = roll_cols(m[0], n), roll_cols(m[1], n)
        re = re + ur * r + ui * i
        im = im + ui * r - ur * i
    return (re, im)


def h_full(h):
    d, r, i = h
    zero = jnp.zeros_like(d[0])
    re = jnp.stack(
        [jnp.stack([d[0], r[0], r[1]]), jnp.stack([r[0], d[1], r[2]]), jnp.stack([r[1], r[2], d[2]])]
    )
    im = jnp.stack(
        [jnp.stack([zero, i[0], i[1]]), jnp.stack([-i[0], zero, i[2]]), jnp.stack([-i[1], -i[2], zero])]
    )
    return (re, im)


def h_sandwich(h, s):
    m = times_h(h_times(h, h_full(s)), h)
    return (
        jnp.stack([m[0][0, 0], m[0][1, 1], m[0][2, 2]]),
        jnp.stack([m[0][0, 1], m[0][0, 2], m[0][1, 2]]),
        jnp.stack([m[1][0, 1], m[1][0, 2], m[1][1, 2]]),
    )


def cooling_pair(g):
    third = (g[0][0] + g[0][1] + g[0][2]) * (1.0 / 3.0)
    d = g[0] - third[None]
    p, q, r = ((g[1][n], g[2][n]) for n in range(3))
    norms = g[1] * g[1] + g[2] * g[2]
    np_, nq, nr = norms[0], norms[1], norms[2]
    d0, d1, d2 = d[0], d[1], d[2]
    s0 = d0 * d0 + np_ + nq
    s1 = d1 * d1 + np_ + nr
    s2 = d2 * d2 + nq + nr
    sp = (q[0] * r[0] + q[1] * r[1] - d2 * p[0], q[1] * r[0] - q[0] * r[1] - d2 * p[1])
    prod = cmul(p, r)
    sq = (prod[0] - d1 * q[0], prod[1] - d1 * q[1])
    sr = (p[0] * q[0] + p[1] * q[1] - d0 * r[0], p[0] * q[1] - p[1] * q[0] - d0 * r[1])
    half = 0.5 * (s0 + s1 + s2)
    det = (
        d0 * d1 * d2
        + 2.0 * (prod[0] * q[0] + prod[1] * q[1])
        - d0 * nr
        - d1 * nq
        - d2 * np_
    )
    a = COOL_SIZE
    linear = (a + (a**3 / 6.0) * half)[None]
    constant = ((a**3 / 6.0) * det)[None]
    even = (
        1.0 + (a * a / 2.0) * jnp.stack([s0, s1, s2]),
        (a * a / 2.0) * jnp.stack([sp[0], sq[0], sr[0]]),
        (a * a / 2.0) * jnp.stack([sp[1], sq[1], sr[1]]),
    )
    odd = (linear * d + constant, linear * g[1], linear * g[2])
    return h_sub(even, odd), h_add(even, odd)


def index_of(axis, ndim):
    return lax.broadcasted_iota(jnp.int32, (1,) * (ndim - 2) + TILE, ndim - 2 + axis)


def shift(x, direction, sign, halo=None):
    n = x.ndim
    if direction == 1:
        return pltpu.roll(x, LANES - NZ if sign > 0 else NZ, n - 1)
    if direction == 2:
        z = index_of(1, n) % NZ
        if sign > 0:
            return jnp.where(
                z == NZ - 1, pltpu.roll(x, NZ - 1, n - 1), pltpu.roll(x, LANES - 1, n - 1)
            )
        return jnp.where(z == 0, pltpu.roll(x, LANES - NZ + 1, n - 1), pltpu.roll(x, 1, n - 1))
    t = index_of(0, n)
    if sign > 0:
        return jnp.where(t == ROWS - 1, halo, pltpu.roll(x, ROWS - 1, n - 2))
    return jnp.where(t == 0, halo, pltpu.roll(x, 1, n - 2))


def m_shift(m, direction, sign, halo=(None, None)):
    return (shift(m[0], direction, sign, halo[0]), shift(m[1], direction, sign, halo[1]))


def h_shift(h, direction, sign, halo=None):
    return h_unpack(shift(h_pack(h), direction, sign, halo))


def unit_where(m, mask):
    one = jnp.where(mask, 1.0, 0.0)
    re = jnp.where(mask, 0.0, m[0])
    im = jnp.where(mask, 0.0, m[1])
    return (add_diagonal(re, one[0, 0]), im)


def time_scan(u, reverse):
    t = index_of(0, 4)
    for step in (1, 2, 4):
        if reverse:
            other = tuple(pltpu.roll(x, ROWS - step, 2) for x in u)
            u = mm(u, unit_where(other, t >= ROWS - step))
        else:
            other = tuple(pltpu.roll(x, step, 2) for x in u)
            u = mm(unit_where(other, t < step), u)
    return u


def kernel(
    sizes,
    u_hbm,
    noise_hbm,
    out_hbm,
    norm_ref,
    u,
    noise,
    inv,
    ahead_x,
    ahead_t,
    qx,
    qx_in,
    qt,
    qt_in,
    slab,
    slabs,
    acc,
    new,
    work,
    final,
    inner,
    inner_in,
    gauge,
    gauge_in,
    norm_tile,
    norm_inner,
    norm_part,
    norm_outer,
    local_sem,
    send_sem,
    recv_sem,
    slab_send,
    slab_recv,
    norm_send,
    norm_recv,
):
    n_ta, n_sa, n_in = sizes
    n_out = n_sa // n_in
    k, j = lax.axis_index("ta"), lax.axis_index("sa")
    j_out, j_in = j // n_in, j % n_in
    t_up, t_down = (lax.rem(k + 1, n_ta), j), (lax.rem(k + n_ta - 1, n_ta), j)
    x_up, x_down = (k, lax.rem(j + 1, n_sa)), (k, lax.rem(j + n_sa - 1, n_sa))
    around = [(lax.rem(k + n_ta - d, n_ta), j) for d in range(1, n_ta)]
    inner_at = [lax.rem(j_in + d, n_in) for d in range(1, n_in)]
    outer_at = [lax.rem(j_out + d, n_out) for d in range(1, n_out)]
    inner_group = [(k, j_out * n_in + at) for at in inner_at]
    outer_group = [(k, at * n_in + j_in) for at in outer_at]

    barrier = pltpu.get_barrier_semaphore()
    partners = around + [x_up, x_down] + inner_group + outer_group
    for device in partners:
        pl.semaphore_signal(barrier, inc=1, device_id=device, device_id_type=MESH)

    loads = [pltpu.make_async_copy(u_hbm.at[d], u.at[d], local_sem.at[d]) for d in range(4)]
    loads.append(pltpu.make_async_copy(noise_hbm, noise, local_sem.at[4]))
    for copy in loads:
        copy.start()

    started = []

    def send(src, dst, device):
        at = len(started)
        copy = pltpu.make_async_remote_copy(
            src_ref=src,
            dst_ref=dst,
            send_sem=send_sem.at[at],
            recv_sem=recv_sem.at[at],
            device_id=device,
            device_id_type=MESH,
        )
        copy.start()
        started.append(copy)
        return copy

    for copy in loads[:4]:
        copy.wait()
    links = [u.at[d] for d in range(4)]
    invs = [inv.at[d] for d in range(4)]
    for d in range(4):
        store(invs[d], adj(load(links[d])))

    def x_corner(nu, halo=(None, None)):
        middle = mm(load(invs[nu]), load(links[0]))
        return mm(m_shift(load(invs[0]), nu, 1, halo), middle)

    store(qx.at[0], x_corner(1))
    store(slab, time_scan(load(links[3]), True))

    pl.semaphore_wait(barrier, len(partners))

    got_ux = {}
    got_qx = {}
    got_ux[3] = send(u.at[3], ahead_x.at[2], x_down)
    got_qx[1] = send(qx.at[0], qx_in.at[0], x_up)
    got_ux[1] = send(u.at[1], ahead_x.at[0], x_down)
    got_ut = send(inv.at[0:3, :, :, :, 0:1, :], ahead_t.at[:, :, :, :, 0:1, :], t_down)
    slab_copies = []
    for d in range(1, n_ta):
        at = d - 1
        row = at // 2
        copy = pltpu.make_async_remote_copy(
            src_ref=slab.at[:, :, :, 0:1, :],
            dst_ref=slabs.at[at % 2, :, :, :, row : row + 1, :],
            send_sem=slab_send.at[at],
            recv_sem=slab_recv.at[at],
            device_id=around[at],
            device_id_type=MESH,
        )
        copy.start()
        slab_copies.append(copy)
    got_ux[2] = send(u.at[2], ahead_x.at[1], x_down)
    store(qx.at[1], x_corner(2))
    got_qx[2] = send(qx.at[1], qx_in.at[1], x_up)

    def t_corner(nu, ahead):
        return mm(mm(load(invs[3]), load(links[nu])), ahead)

    got_qt = {}
    for nu in (1, 2):
        store(qt.at[nu], t_corner(nu, m_shift(load(links[3]), nu, 1)))
    got_qt[1] = send(qt.at[1:3, :, :, :, 7:8, :], qt_in.at[1:3, :, :, :, 7:8, :], t_up)

    u_1, u_2 = load(links[1]), load(links[2])
    n_12 = mm(m_shift(u_2, 1, 1), m_shift(load(invs[1]), 2, 1))
    m_12 = mm(load(invs[2]), u_1)
    a_12 = less_inverse(mm(u_1, mm(n_12, load(invs[2]))))
    store(acc.at[1], sub(a_12, m_shift(less_inverse(mm(m_12, n_12)), 2, -1)))
    store(acc.at[2], sub(m_shift(less_inverse(mm(n_12, m_12)), 1, -1), a_12))

    got_ut.wait_recv()

    def inv_ahead(nu):
        return (ahead_t[nu, 0, :, :, 0:1, :], ahead_t[nu, 1, :, :, 0:1, :])

    store(qx.at[2], x_corner(3, inv_ahead(0)))
    got_qx[3] = send(qx.at[2], qx_in.at[2], x_up)

    def accumulate(d, term, sign):
        now = load(acc.at[d])
        store(acc.at[d], add(now, term) if sign > 0 else sub(now, term))

    got_qt[1].wait_recv()

    def behind_t(nu):
        return (qt_in[nu, 0, :, :, 7:8, :], qt_in[nu, 1, :, :, 7:8, :])

    for nu in (1, 2):
        n_nt = mm(m_shift(load(links[3]), nu, 1), m_shift(load(invs[nu]), 3, 1, inv_ahead(nu)))
        a_nt = less_inverse(mm(load(links[nu]), mm(n_nt, load(invs[3]))))
        m_nt = mm(load(invs[3]), load(links[nu]))
        lower = mm(m_shift(load(qt.at[nu]), 3, -1, behind_t(nu)), load(invs[nu]))
        accumulate(nu, sub(a_nt, less_inverse(lower)), 1)
        to_t = sub(m_shift(less_inverse(mm(n_nt, m_nt)), nu, -1), a_nt)
        if nu == 1:
            store(acc.at[3], to_t)
        else:
            accumulate(3, to_t, 1)

    got_ux[3].wait_recv()
    store(qt.at[0], t_corner(0, load(ahead_x.at[2])))
    got_qt[0] = send(qt.at[0, :, :, :, 7:8, :], qt_in.at[0, :, :, :, 7:8, :], t_up)

    prefix = time_scan(load(links[3]), False)
    first = index_of(0, 4) == 0
    prefix = unit_where(tuple(pltpu.roll(x, 1, 2) for x in prefix), first)
    for copy in slab_copies:
        copy.wait_recv()
    slot = 2 * index_of(0, 4)
    even, odd = load(slabs.at[0]), load(slabs.at[1])
    if n_ta - 1 < 2 * ROWS - 1:
        even = unit_where(even, slot >= n_ta - 1)
    odd = unit_where(odd, slot + 1 >= n_ta - 1)
    others = mm(even, odd)
    for step in (1, 2, 4):
        others = mm(others, tuple(pltpu.roll(x, ROWS - step, 2) for x in others))
    others = tuple(jnp.broadcast_to(x[:, :, 0:1, :], x.shape) for x in others)
    line = mm(mm(load(slab), others), prefix)
    back = adj(line)
    former = (add_diagonal(FUGACITY * line[0], 1.0), FUGACITY * line[1])
    latter = (add_diagonal(ANTI_FUGACITY * back[0], 1.0), ANTI_FUGACITY * back[1])
    drift = sub(inverse(latter), inverse(former))
    weight = 4.0 * 3.0 / COUPLING
    accumulate(3, (weight * drift[0], weight * drift[1]), 1)

    for nu in (3, 1, 2):
        if nu != 3:
            got_ux[nu].wait_recv()
        halo = inv_ahead(0) if nu == 3 else (None, None)
        n_xn = mm(load(ahead_x.at[nu - 1]), m_shift(load(invs[0]), nu, 1, halo))
        a_xn = less_inverse(mm(load(links[0]), mm(n_xn, load(invs[nu]))))
        if nu == 3:
            store(acc.at[0], a_xn)
        else:
            m_xn = mm(load(invs[nu]), load(links[0]))
            lower = m_shift(less_inverse(mm(m_xn, n_xn)), nu, -1)
            accumulate(0, sub(a_xn, lower), 1)
        accumulate(nu, a_xn, -1)

    got_qt[0].wait_recv()
    lower = mm(m_shift(load(qt.at[0]), 3, -1, behind_t(0)), load(invs[0]))
    accumulate(0, less_inverse(lower), -1)

    loads[4].wait()
    c = math.sqrt(STEP_SIZE)

    def update(d):
        x = load(acc.at[d])
        w = -STEP_SIZE * COUPLING / 3.0
        mean_r = (x[0][0, 0] + x[0][1, 1] + x[0][2, 2]) * (1.0 / 3.0)
        mean_i = (x[1][0, 0] + x[1][1, 1] + x[1][2, 2]) * (1.0 / 3.0)
        n = [c * noise[d, a] for a in range(8)]
        n7 = n[7] * (1.0 / math.sqrt(3.0))
        real = {(0, 1): n[1], (0, 2): n[4], (1, 2): n[6]}
        imag = {(0, 1): n[0], (0, 2): n[3], (1, 2): n[5]}
        diag = (n[2] + n7, n7 - n[2], -2.0 * n7)
        yr, yi = [], []
        for a in range(3):
            row_r, row_i = [], []
            for b in range(3):
                if a == b:
                    row_r.append(w * (x[0][a, b] - mean_r))
                    row_i.append(w * (x[1][a, b] - mean_i) + diag[a])
                elif a < b:
                    row_r.append(w * x[0][a, b] + real[a, b])
                    row_i.append(w * x[1][a, b] + imag[a, b])
                else:
                    row_r.append(w * x[0][a, b] - real[b, a])
                    row_i.append(w * x[1][a, b] + imag[b, a])
            yr.append(jnp.stack(row_r))
            yi.append(jnp.stack(row_i))
        m = exp_times((jnp.stack(yr), jnp.stack(yi)), load(links[d]))
        store(new.at[d], m)
        return m

    m = update(0)
    inner[0] = h_pack(gram_cols(m))
    got_inner_x = send(inner.at[0], inner_in.at[0], x_up)
    plus = gram_rows(m)
    for nu in (1, 2, 3):
        got_qx[nu].wait_recv()
        accumulate(nu, less_inverse(mm(load(links[nu]), load(qx_in.at[nu - 1]))), 1)
        if nu == 3:
            m = update(3)
            inner[1] = h_pack(gram_cols(m))
            got_inner_t = send(inner.at[1, :, 7:8, :], inner_in.at[1, :, 7:8, :], t_up)
            plus = h_add(plus, gram_rows(m))
    minus = None
    for d in (1, 2):
        m = update(d)
        plus = h_add(plus, gram_rows(m))
        lagged = h_shift(gram_cols(m), d, -1)
        minus = lagged if minus is None else h_add(minus, lagged)
    norms = [plus[0][0] + plus[0][1] + plus[0][2]]
    got_inner_t.wait_recv()
    minus = h_add(minus, h_unpack(shift(inner[1], 3, -1, inner_in[1, :, 7:8, :])))
    got_inner_x.wait_recv()
    minus = h_add(minus, h_unpack(inner_in[0]))

    low, high = cooling_pair(h_sub(plus, minus))
    gauge[0] = h_pack(high)
    got_high_x = send(gauge.at[0], gauge_in.at[0], x_down)
    got_high_t = send(gauge.at[0, :, 0:1, :], gauge_in.at[1, :, 0:1, :], t_down)

    m = h_times(low, load(new.at[0]))
    store(work.at[0], m)
    inner[2] = h_pack(gram_cols(m))
    got_inner_x = send(inner.at[2], inner_in.at[2], x_up)
    m = h_times(low, load(new.at[3]))
    store(work.at[3], m)
    inner[3] = h_pack(gram_cols(m))
    got_inner_t = send(inner.at[3, :, 7:8, :], inner_in.at[3, :, 7:8, :], t_up)
    plus = minus = None
    for d in (1, 2):
        m = h_times(low, load(new.at[d]))
        lagged = h_shift(gram_cols(m), d, -1)
        minus = lagged if minus is None else h_add(minus, lagged)
        m = times_h(m, h_shift(high, d, 1))
        store(new.at[d], m)
        plus = gram_rows(m) if plus is None else h_add(plus, gram_rows(m))
    got_high_t.wait_recv()
    m = times_h(load(work.at[3]), h_unpack(shift(gauge[0], 3, 1, gauge_in[1, :, 0:1, :])))
    store(new.at[3], m)
    plus = h_add(plus, gram_rows(m))
    got_inner_t.wait_recv()
    minus = h_add(minus, h_unpack(shift(inner[3], 3, -1, inner_in[3, :, 7:8, :])))
    got_high_x.wait_recv()
    m = times_h(load(work.at[0]), h_unpack(gauge_in[0]))
    store(new.at[0], m)
    plus = h_add(plus, gram_rows(m))
    norms.append(plus[0][0] + plus[0][1] + plus[0][2])
    got_inner_x.wait_recv()
    minus = h_add(minus, h_unpack(inner_in[2]))
    minus = h_sandwich(h_unpack(gauge[0]), minus)

    low, high = cooling_pair(h_sub(plus, minus))
    gauge[1] = h_pack(high)
    got_high_x = send(gauge.at[1], gauge_in.at[2], x_down)
    got_high_t = send(gauge.at[1, :, 0:1, :], gauge_in.at[3, :, 0:1, :], t_down)
    total = None
    writes = []

    def finish(d, m, total):
        store(final.at[d], m)
        copy = pltpu.make_async_copy(final.at[d], out_hbm.at[d], local_sem.at[d])
        copy.start()
        writes.append(copy)
        squares = m[0] * m[0] + m[1] * m[1]
        squares = squares[0] + squares[1] + squares[2]
        squares = squares[0] + squares[1] + squares[2]
        return squares if total is None else total + squares

    for d in (1, 2):
        m = times_h(h_times(low, load(new.at[d])), h_shift(high, d, 1))
        total = finish(d, m, total)
    last_t = h_times(low, load(new.at[3]))
    store(work.at[0], h_times(low, load(new.at[0])))
    got_high_t.wait_recv()
    m = times_h(last_t, h_unpack(shift(gauge[1], 3, 1, gauge_in[3, :, 0:1, :])))
    total = finish(3, m, total)
    got_high_x.wait_recv()
    total = finish(0, times_h(load(work.at[0]), h_unpack(gauge_in[2])), total)
    norms.append(total)

    row, lane = index_of(0, 2), index_of(1, 2)
    tile = jnp.zeros(TILE, jnp.float32)
    for at, value in enumerate(norms):
        sums = jnp.sum(value, axis=1, keepdims=True)
        as_row = jnp.sum(jnp.where(row == lane, sums, 0.0), axis=0, keepdims=True)
        tile = jnp.where(row == at, as_row, tile)

    def summed(tile, src, buffer, mine, others_at, group, sem0):
        src[...] = tile
        buffer[mine] = tile
        copies = []
        for d, device in enumerate(group):
            copy = pltpu.make_async_remote_copy(
                src_ref=src,
                dst_ref=buffer.at[mine],
                send_sem=norm_send.at[sem0 + d],
                recv_sem=norm_recv.at[sem0 + mine],
                device_id=device,
                device_id_type=MESH,
            )
            copy.start()
            copies.append(copy)
        for d, device in enumerate(group):
            pltpu.make_async_remote_copy(
                src_ref=src,
                dst_ref=buffer.at[others_at[d]],
                send_sem=norm_send.at[sem0 + d],
                recv_sem=norm_recv.at[sem0 + others_at[d]],
                device_id=device,
                device_id_type=MESH,
            ).wait_recv()
        result = buffer[0]
        for at in range(1, len(group) + 1):
            result = result + buffer[at]
        return result, copies

    tile, copies = summed(tile, norm_tile, norm_inner, j_in, inner_at, inner_group, 0)
    started.extend(copies)
    tile, copies = summed(tile, norm_part, norm_outer, j_out, outer_at, outer_group, n_in)
    started.extend(copies)
    site_count = n_sa * LANES
    norm_ref[...] = tile[0:3, 0:ROWS] * (1.0 / (4.0 * site_count)) - 3.0

    for copy in started + slab_copies:
        copy.wait_send()
    for copy in writes:
        copy.wait()


def local(gauge_links, noise_field):
    n_ta, n_sa = lax.axis_size("ta"), lax.axis_size("sa")
    n_in = max(n_sa // 4, 2)
    n_out = n_sa // n_in
    shape = (4,) + MAT
    vmem = lambda *s: pltpu.VMEM(s, jnp.float32)
    dma = lambda n: pltpu.SemaphoreType.DMA((n,))
    cooled, norms = pl.pallas_call(
        functools.partial(kernel, (n_ta, n_sa, n_in)),
        out_shape=(
            jax.ShapeDtypeStruct(shape, jnp.float32),
            jax.ShapeDtypeStruct((3, ROWS), jnp.float32),
        ),
        in_specs=[pl.BlockSpec(memory_space=pl.ANY)] * 2,
        out_specs=(
            pl.BlockSpec(memory_space=pl.ANY),
            pl.BlockSpec(memory_space=pltpu.VMEM),
        ),
        scratch_shapes=[
            vmem(*shape),
            vmem(4, 8, *TILE),
            vmem(*shape),
            vmem(3, *MAT),
            vmem(3, *MAT),
            vmem(3, *MAT),
            vmem(3, *MAT),
            vmem(3, *MAT),
            vmem(3, *MAT),
            vmem(*MAT),
            vmem(2, *MAT),
            vmem(*shape),
            vmem(*shape),
            vmem(*shape),
            vmem(*shape),
            vmem(4, *HERM),
            vmem(4, *HERM),
            vmem(2, *HERM),
            vmem(4, *HERM),
            vmem(*TILE),
            vmem(n_in, *TILE),
            vmem(*TILE),
            vmem(n_out, *TILE),
            dma(5),
            dma(24),
            dma(24),
            dma(n_ta - 1),
            dma(n_ta - 1),
            dma(n_in + n_out),
            dma(n_in + n_out),
        ],
        compiler_params=pltpu.CompilerParams(
            collective_id=0, has_side_effects=True, vmem_limit_bytes=32 * 1024 * 1024
        ),
        name="langevin_step",
    )(gauge_links.reshape(shape), noise_field.reshape((4, 8) + TILE))
    return cooled.reshape(gauge_links.shape), norms


def solution(mesh):
    placed = (P(None, None, None, None, "sa", "ta", None), P(None, None, "sa", "ta", None))
    return jax.shard_map(
        local,
        mesh=mesh,
        in_specs=placed,
        out_specs=(P(None, None, None, None, "sa", "ta", None), P(None, "ta")),
        check_vma=False,
    )
```

```python
import functools
import math

import jax
import jax.numpy as jnp
from jax import lax
from jax.experimental import pallas as pl
from jax.experimental.pallas import tpu as pltpu
from jax.sharding import PartitionSpec as P

NY = 8
NZ = 16
LANES = NY * NZ
ROWS = 8

COUPLING = 5.6
STEP_SIZE = 0.02
COOL_SIZE = 0.02
FUGACITY = 0.5
ANTI_FUGACITY = 0.02

MESH = pl.DeviceIdType.MESH
VMEM_LIMIT = 32 * 1024 * 1024
TILE = (ROWS, LANES)
MATRIX = (3, 3) + TILE
MAT = 18
HERM = 9


def load(ref):
    return (ref[0:9].reshape(MATRIX), ref[9:18].reshape(MATRIX))


def load_row(ref, row):
    shape = (3, 3, 1, LANES)
    return tuple(ref[9 * c : 9 * c + 9, row : row + 1, :].reshape(shape) for c in range(2))


def store(ref, m):
    ref[0:9] = m[0].reshape((9,) + TILE)
    ref[9:18] = m[1].reshape((9,) + TILE)


def matrix_at(ref, at):
    return ref.at[MAT * at : MAT * (at + 1)]


def herm_at(ref, at):
    return ref.at[HERM * at : HERM * (at + 1)]


def row_of(ref, row):
    return ref.at[:, row : row + 1, :]


def add(a, b):
    return (a[0] + b[0], a[1] + b[1])


def sub(a, b):
    return (a[0] - b[0], a[1] - b[1])


def mm(a, b):
    ar, ai = a
    br, bi = b
    re = im = None
    for k in range(3):
        cr, ci = ar[:, k : k + 1], ai[:, k : k + 1]
        rr, ri = br[k : k + 1], bi[k : k + 1]
        tr = cr * rr - ci * ri
        ti = cr * ri + ci * rr
        re = tr if re is None else re + tr
        im = ti if im is None else im + ti
    return (re, im)


def roll_rows(x, n):
    return jnp.concatenate([x[n:], x[:n]], axis=0)


def roll_cols(x, n):
    return jnp.concatenate([x[:, n:], x[:, :n]], axis=1)


def transposed(x):
    return jnp.stack([x[:, i] for i in range(3)])


def cmul(a, b):
    return (a[0] * b[0] - a[1] * b[1], a[0] * b[1] + a[1] * b[0])


def adj(m):
    one = tuple(roll_rows(x, 1) for x in m)
    two = tuple(roll_rows(x, 2) for x in m)
    plus = cmul(tuple(roll_cols(x, 1) for x in one), tuple(roll_cols(x, 2) for x in two))
    minus = cmul(tuple(roll_cols(x, 2) for x in one), tuple(roll_cols(x, 1) for x in two))
    return (transposed(plus[0] - minus[0]), transposed(plus[1] - minus[1]))


def less_inverse(p):
    return sub(p, adj(p))


def entry(m, i, j):
    return (m[0][i, j], m[1][i, j])


def add_diagonal(x, value):
    rows = []
    for i in range(3):
        parts = [(x[i, i] + value)[None]]
        if i > 0:
            parts.insert(0, x[i, :i])
        if i < 2:
            parts.append(x[i, i + 1 :])
        rows.append(jnp.concatenate(parts, axis=0))
    return jnp.stack(rows)


def inverse(m):
    a = adj(m)
    det = cmul(entry(m, 0, 0), entry(a, 0, 0))
    for j in (1, 2):
        det = add(det, cmul(entry(m, 0, j), entry(a, j, 0)))
    scale = 1.0 / (det[0] * det[0] + det[1] * det[1])
    factor = ((det[0] * scale)[None, None], (-det[1] * scale)[None, None])
    return cmul(a, factor)


def exp_times(y, u):
    square = mm(y, y)
    trace = tuple(x[0, 0] + x[1, 1] + x[2, 2] for x in square)
    det = None
    for j in range(3):
        a, b = (j + 1) % 3, (j + 2) % 3
        minor = sub(
            cmul(entry(y, 1, a), entry(y, 2, b)), cmul(entry(y, 1, b), entry(y, 2, a))
        )
        term = cmul(entry(y, 0, j), minor)
        det = term if det is None else add(det, term)
    beta = ((1.0 + trace[0] * (1.0 / 12.0))[None, None], (trace[1] * (1.0 / 12.0))[None, None])
    linear = cmul(y, beta)
    re = add_diagonal(linear[0] + 0.5 * square[0], 1.0 + det[0] * (1.0 / 6.0))
    im = add_diagonal(linear[1] + 0.5 * square[1], det[1] * (1.0 / 6.0))
    return mm((re, im), u)


def gram_rows(m):
    re, im = m
    diag = re * re + im * im
    a = tuple(jnp.concatenate([x[0:1], x[0:1], x[1:2]], axis=0) for x in m)
    b = tuple(jnp.concatenate([x[1:2], x[2:3], x[2:3]], axis=0) for x in m)
    pr = a[0] * b[0] + a[1] * b[1]
    pi = a[1] * b[0] - a[0] * b[1]
    return tuple(x[:, 0] + x[:, 1] + x[:, 2] for x in (diag, pr, pi))


def gram_cols(m):
    re, im = m
    diag = re * re + im * im
    a = tuple(jnp.concatenate([x[:, 0:1], x[:, 0:1], x[:, 1:2]], axis=1) for x in m)
    b = tuple(jnp.concatenate([x[:, 1:2], x[:, 2:3], x[:, 2:3]], axis=1) for x in m)
    pr = a[0] * b[0] + a[1] * b[1]
    pi = a[0] * b[1] - a[1] * b[0]
    return tuple(x[0] + x[1] + x[2] for x in (diag, pr, pi))


def h_add(a, b):
    return tuple(x + y for x, y in zip(a, b))


def h_sub(a, b):
    return tuple(x - y for x, y in zip(a, b))


def h_pack(h):
    return jnp.concatenate(h, axis=0)


def h_unpack(x):
    return (x[0:3], x[3:6], x[6:9])


def h_offsets(h):
    _, r, i = h
    one = (jnp.stack([r[0], r[2], r[1]]), jnp.stack([i[0], i[2], -i[1]]))
    two = (jnp.stack([r[1], r[0], r[2]]), jnp.stack([i[1], -i[0], -i[2]]))
    return one, two


def h_times(h, m):
    d = h[0][:, None]
    one, two = h_offsets(h)
    re, im = d * m[0], d * m[1]
    for n, off in ((1, one), (2, two)):
        r, i = off[0][:, None], off[1][:, None]
        ur, ui = roll_rows(m[0], n), roll_rows(m[1], n)
        re = re + r * ur - i * ui
        im = im + r * ui + i * ur
    return (re, im)


def times_h(m, h):
    d = h[0][None]
    one, two = h_offsets(h)
    re, im = m[0] * d, m[1] * d
    for n, off in ((1, one), (2, two)):
        r, i = off[0][None], off[1][None]
        ur, ui = roll_cols(m[0], n), roll_cols(m[1], n)
        re = re + ur * r + ui * i
        im = im + ui * r - ur * i
    return (re, im)


def h_full(h):
    d, r, i = h
    zero = jnp.zeros_like(d[0])
    re = jnp.stack(
        [jnp.stack([d[0], r[0], r[1]]), jnp.stack([r[0], d[1], r[2]]), jnp.stack([r[1], r[2], d[2]])]
    )
    im = jnp.stack(
        [jnp.stack([zero, i[0], i[1]]), jnp.stack([-i[0], zero, i[2]]), jnp.stack([-i[1], -i[2], zero])]
    )
    return (re, im)


def h_sandwich(h, s):
    m = times_h(h_times(h, h_full(s)), h)
    return (
        jnp.stack([m[0][0, 0], m[0][1, 1], m[0][2, 2]]),
        jnp.stack([m[0][0, 1], m[0][0, 2], m[0][1, 2]]),
        jnp.stack([m[1][0, 1], m[1][0, 2], m[1][1, 2]]),
    )


def cooling_pair(g):
    third = (g[0][0] + g[0][1] + g[0][2]) * (1.0 / 3.0)
    d = g[0] - third[None]
    p, q, r = ((g[1][n], g[2][n]) for n in range(3))
    norms = g[1] * g[1] + g[2] * g[2]
    np_, nq, nr = norms[0], norms[1], norms[2]
    d0, d1, d2 = d[0], d[1], d[2]
    s0 = d0 * d0 + np_ + nq
    s1 = d1 * d1 + np_ + nr
    s2 = d2 * d2 + nq + nr
    sp = (q[0] * r[0] + q[1] * r[1] - d2 * p[0], q[1] * r[0] - q[0] * r[1] - d2 * p[1])
    prod = cmul(p, r)
    sq = (prod[0] - d1 * q[0], prod[1] - d1 * q[1])
    sr = (p[0] * q[0] + p[1] * q[1] - d0 * r[0], p[0] * q[1] - p[1] * q[0] - d0 * r[1])
    half = 0.5 * (s0 + s1 + s2)
    det = (
        d0 * d1 * d2
        + 2.0 * (prod[0] * q[0] + prod[1] * q[1])
        - d0 * nr
        - d1 * nq
        - d2 * np_
    )
    a = COOL_SIZE
    linear = (a + (a**3 / 6.0) * half)[None]
    constant = ((a**3 / 6.0) * det)[None]
    even = (
        1.0 + (a * a / 2.0) * jnp.stack([s0, s1, s2]),
        (a * a / 2.0) * jnp.stack([sp[0], sq[0], sr[0]]),
        (a * a / 2.0) * jnp.stack([sp[1], sq[1], sr[1]]),
    )
    odd = (linear * d + constant, linear * g[1], linear * g[2])
    return h_sub(even, odd), h_add(even, odd)


def index_of(axis, ndim):
    return lax.broadcasted_iota(jnp.int32, (1,) * (ndim - 2) + TILE, ndim - 2 + axis)


def shift(x, direction, sign, halo=None):
    n = x.ndim
    if direction == 1:
        return pltpu.roll(x, LANES - NZ if sign > 0 else NZ, n - 1)
    if direction == 2:
        z = index_of(1, n) % NZ
        if sign > 0:
            return jnp.where(
                z == NZ - 1, pltpu.roll(x, NZ - 1, n - 1), pltpu.roll(x, LANES - 1, n - 1)
            )
        return jnp.where(z == 0, pltpu.roll(x, LANES - NZ + 1, n - 1), pltpu.roll(x, 1, n - 1))
    t = index_of(0, n)
    if sign > 0:
        return jnp.where(t == ROWS - 1, halo, pltpu.roll(x, ROWS - 1, n - 2))
    return jnp.where(t == 0, halo, pltpu.roll(x, 1, n - 2))


def m_shift(m, direction, sign, halo=(None, None)):
    return (shift(m[0], direction, sign, halo[0]), shift(m[1], direction, sign, halo[1]))


def h_shift(h, direction, sign, halo=None):
    return h_unpack(shift(h_pack(h), direction, sign, halo))


def unit_where(m, mask):
    one = jnp.where(mask, 1.0, 0.0)
    re = jnp.where(mask, 0.0, m[0])
    im = jnp.where(mask, 0.0, m[1])
    return (add_diagonal(re, one[0, 0]), im)


def time_scan(u, reverse):
    t = index_of(0, 4)
    for step in (1, 2, 4):
        if reverse:
            other = tuple(pltpu.roll(x, ROWS - step, 2) for x in u)
            u = mm(u, unit_where(other, t >= ROWS - step))
        else:
            other = tuple(pltpu.roll(x, step, 2) for x in u)
            u = mm(unit_where(other, t < step), u)
    return u


def far_first(n_out, n_in):
    steps = [(a, b) for a in range(n_out) for b in range(n_in) if a or b]
    return sorted(steps, key=lambda s: -(min(s[0], n_out - s[0]) + min(s[1], n_in - s[1])))


def kernel(
    sizes,
    u_hbm,
    noise_hbm,
    out,
    norm_ref,
    u,
    noise,
    inv,
    ahead_x,
    ahead_t,
    ahead_xt,
    behind_xt,
    qx,
    qx_in,
    qt,
    qt_in,
    slab,
    slabs,
    prefix,
    acc,
    new,
    gx,
    gx_in,
    gt,
    gt_in,
    part,
    part_in,
    norm_row,
    norm_rows,
    local_sem,
    send_sem,
    recv_sem,
    slab_send,
    slab_recv,
    norm_send,
    norm_recv,
):
    n_ta, n_sa, n_in = sizes
    n_out = n_sa // n_in
    k, j = lax.axis_index("ta"), lax.axis_index("sa")
    j_out, j_in = j // n_in, j % n_in
    k_up, k_down = lax.rem(k + 1, n_ta), lax.rem(k + n_ta - 1, n_ta)
    j_up, j_down = lax.rem(j + 1, n_sa), lax.rem(j + n_sa - 1, n_sa)
    t_up, t_down, x_up, x_down = (k_up, j), (k_down, j), (k, j_up), (k, j_down)
    x_up_t_down, x_down_t_up = (k_down, j_up), (k_up, j_down)
    around = [lax.rem(k + n_ta - d, n_ta) for d in range(1, n_ta)]
    group = [
        lax.rem(j_out + a, n_out) * n_in + lax.rem(j_in + b, n_in)
        for a, b in far_first(n_out, n_in)
    ]

    barrier = pltpu.get_barrier_semaphore()
    partners = [
        (min(a, n_out - a) + min(b, n_in - b), (k, at))
        for (a, b), at in zip(far_first(n_out, n_in), group)
    ]
    partners += [(min(d, n_ta - d) / 2, (at, j)) for d, at in enumerate(around, 1)]
    partners += [(2.5, x_up_t_down), (2.5, x_down_t_up)]
    partners = [device for _, device in sorted(partners, key=lambda p: -p[0])]
    for device in partners:
        pl.semaphore_signal(barrier, inc=1, device_id=device, device_id_type=MESH)

    loads = [pltpu.make_async_copy(matrix_at(u_hbm, d), matrix_at(u, d), local_sem.at[d]) for d in range(4)]
    loads.append(pltpu.make_async_copy(noise_hbm, noise, local_sem.at[4]))
    for copy in loads:
        copy.start()

    started = []

    def send(src, dst, device):
        at = len(started)
        copy = pltpu.make_async_remote_copy(
            src_ref=src,
            dst_ref=dst,
            send_sem=send_sem.at[at],
            recv_sem=recv_sem.at[at],
            device_id=device,
            device_id_type=MESH,
        )
        copy.start()
        started.append(copy)
        return copy

    def accumulate(d, term, sign):
        now = load(matrix_at(acc, d))
        store(matrix_at(acc, d), add(now, term) if sign > 0 else sub(now, term))


    links = [matrix_at(u, d) for d in range(4)]
    invs = [matrix_at(inv, d) for d in range(4)]
    t_of = index_of(0, 4)
    for d in range(4):
        loads[d].wait()
        store(invs[d], adj(load(links[d])))

    for nu in (1, 2):
        middle = mm(load(invs[nu]), load(links[0]))
        store(matrix_at(qx, nu - 1), mm(m_shift(load(invs[0]), nu, 1), middle))
    middle = mm(load(invs[3]), load(links[0]))
    store(matrix_at(qt, 0), middle)
    raised = tuple(pltpu.roll(x, ROWS - 1, 2) for x in load(invs[0]))
    whole = mm(raised, middle)
    store(matrix_at(qx, 2), tuple(jnp.where(t_of == ROWS - 1, b, a) for a, b in zip(whole, middle)))

    for nu in (1, 2):
        store(matrix_at(qt, nu), mm(mm(load(invs[3]), load(links[nu])), m_shift(load(links[3]), nu, 1)))

    store(slab, time_scan(load(links[3]), True))
    scan = time_scan(load(links[3]), False)
    store(prefix, unit_where(tuple(pltpu.roll(x, 1, 2) for x in scan), t_of == 0))

    u_1, u_2 = load(links[1]), load(links[2])
    n_12 = mm(m_shift(u_2, 1, 1), m_shift(load(invs[1]), 2, 1))
    m_12 = mm(load(invs[2]), u_1)
    a_12 = less_inverse(mm(u_1, mm(n_12, load(invs[2]))))
    store(matrix_at(acc, 1), sub(a_12, m_shift(less_inverse(mm(m_12, n_12)), 2, -1)))
    store(matrix_at(acc, 2), sub(m_shift(less_inverse(mm(n_12, m_12)), 1, -1), a_12))


    pl.semaphore_wait(barrier, len(partners))

    got_ux, got_qx = {}, {}
    for nu in (3, 1, 2):
        got_ux[nu] = send(links[nu], matrix_at(ahead_x, nu - 1), x_down)
        got_qx[nu] = send(matrix_at(qx, nu - 1), matrix_at(qx_in, nu - 1), x_up)
    got_ut = send(inv.at[0 : 3 * MAT, 0:1, :], row_of(ahead_t, 0), t_down)
    got_qt = send(row_of(qt, 7), row_of(qt_in, 7), t_up)
    slab_copies = []
    far_order = sorted(range(1, n_ta), key=lambda d: -min(d, n_ta - d))
    for d in far_order:
        at = d - 1
        row = at // 2
        copy = pltpu.make_async_remote_copy(
            src_ref=row_of(slab, 0),
            dst_ref=row_of(matrix_at(slabs, at % 2), row),
            send_sem=slab_send.at[at],
            recv_sem=slab_recv.at[at],
            device_id=(around[at], j),
            device_id_type=MESH,
        )
        copy.start()
        slab_copies.append(copy)
    got_inv_xt = send(row_of(invs[0], 0), row_of(ahead_xt, 0), x_up_t_down)
    got_u_xt = send(row_of(links[3], 7), row_of(behind_xt, 7), x_down_t_up)

    got_ut.wait_recv()

    def inv_ahead(nu):
        return load_row(matrix_at(ahead_t, nu), 0)

    got_qt.wait_recv()

    def behind_t(nu):
        return load_row(matrix_at(qt_in, nu), 7)

    for nu in (1, 2):
        n_nt = mm(m_shift(load(links[3]), nu, 1), m_shift(load(invs[nu]), 3, 1, inv_ahead(nu)))
        a_nt = less_inverse(mm(load(links[nu]), mm(n_nt, load(invs[3]))))
        m_nt = mm(load(invs[3]), load(links[nu]))
        lower = mm(m_shift(load(matrix_at(qt, nu)), 3, -1, behind_t(nu)), load(invs[nu]))
        accumulate(nu, sub(a_nt, less_inverse(lower)), 1)
        to_t = sub(m_shift(less_inverse(mm(n_nt, m_nt)), nu, -1), a_nt)
        if nu == 1:
            store(matrix_at(acc, 3), to_t)
        else:
            accumulate(3, to_t, 1)

    for copy in slab_copies:
        copy.wait_recv()
    slot = 2 * t_of
    even, odd = load(matrix_at(slabs, 0)), load(matrix_at(slabs, 1))
    if n_ta - 1 < 2 * ROWS - 1:
        even = unit_where(even, slot >= n_ta - 1)
    odd = unit_where(odd, slot + 1 >= n_ta - 1)
    others = mm(even, odd)
    for step in (1, 2, 4):
        others = mm(others, tuple(pltpu.roll(x, ROWS - step, 2) for x in others))
    others = tuple(jnp.broadcast_to(x[:, :, 0:1, :], x.shape) for x in others)
    line = mm(mm(load(slab), others), load(prefix))
    back = adj(line)
    former = (add_diagonal(FUGACITY * line[0], 1.0), FUGACITY * line[1])
    latter = (add_diagonal(ANTI_FUGACITY * back[0], 1.0), ANTI_FUGACITY * back[1])
    drift = sub(inverse(latter), inverse(former))
    weight = 4.0 * 3.0 / COUPLING
    accumulate(3, (weight * drift[0], weight * drift[1]), 1)

    for nu in (3, 1, 2):
        got_ux[nu].wait_recv()
        halo = inv_ahead(0) if nu == 3 else (None, None)
        n_xn = mm(load(matrix_at(ahead_x, nu - 1)), m_shift(load(invs[0]), nu, 1, halo))
        a_xn = less_inverse(mm(load(links[0]), mm(n_xn, load(invs[nu]))))
        if nu == 3:
            got_u_xt.wait_recv()
            ahead = load_row(behind_xt, 7)
            corner = mm(load(matrix_at(qt, 0)), load(matrix_at(ahead_x, 2)))
            corner = m_shift(corner, 3, -1, mm(behind_t(0), ahead))
            store(matrix_at(acc, 0), sub(a_xn, less_inverse(mm(corner, load(invs[0])))))
        else:
            m_xn = mm(load(invs[nu]), load(links[0]))
            lower = m_shift(less_inverse(mm(m_xn, n_xn)), nu, -1)
            accumulate(0, sub(a_xn, lower), 1)
        got_qx[nu].wait_recv()
        corner = load(matrix_at(qx_in, nu - 1))
        if nu == 3:
            got_inv_xt.wait_recv()
            ahead = load_row(ahead_xt, 0)
            fixed = mm(ahead, corner)
            corner = tuple(jnp.where(t_of == ROWS - 1, b, a) for a, b in zip(corner, fixed))
        accumulate(nu, sub(less_inverse(mm(load(links[nu]), corner)), a_xn), 1)

    loads[4].wait()
    c = math.sqrt(STEP_SIZE)

    def update(d):
        x = load(matrix_at(acc, d))
        w = -STEP_SIZE * COUPLING / 3.0
        mean_r = (x[0][0, 0] + x[0][1, 1] + x[0][2, 2]) * (1.0 / 3.0)
        mean_i = (x[1][0, 0] + x[1][1, 1] + x[1][2, 2]) * (1.0 / 3.0)
        n = [c * noise[d, a] for a in range(8)]
        n7 = n[7] * (1.0 / math.sqrt(3.0))
        real = {(0, 1): n[1], (0, 2): n[4], (1, 2): n[6]}
        imag = {(0, 1): n[0], (0, 2): n[3], (1, 2): n[5]}
        diag = (n[2] + n7, n7 - n[2], -2.0 * n7)
        yr, yi = [], []
        for a in range(3):
            row_r, row_i = [], []
            for b in range(3):
                if a == b:
                    row_r.append(w * (x[0][a, b] - mean_r))
                    row_i.append(w * (x[1][a, b] - mean_i) + diag[a])
                elif a < b:
                    row_r.append(w * x[0][a, b] + real[a, b])
                    row_i.append(w * x[1][a, b] + imag[a, b])
                else:
                    row_r.append(w * x[0][a, b] - real[b, a])
                    row_i.append(w * x[1][a, b] + imag[b, a])
            yr.append(jnp.stack(row_r))
            yi.append(jnp.stack(row_i))
        return exp_times((jnp.stack(yr), jnp.stack(yi)), load(links[d]))


    def exchange(step, link):
        m = link(0)
        plus = gram_rows(m)
        herm_at(gx, step)[...] = h_pack(gram_cols(m))
        got = [send(herm_at(gx, step), herm_at(gx_in, step), x_up)]
        got.append(send(row_of(herm_at(gx, step), 0), row_of(herm_at(gx_in, 2 + step), 0), x_up_t_down))
        m = link(3)
        plus = h_add(plus, gram_rows(m))
        columns = h_pack(gram_cols(m))
        herm_at(gt, step)[...] = columns
        got.append(send(row_of(herm_at(gt, step), 7), row_of(herm_at(gt_in, step), 7), t_up))
        got.append(send(row_of(herm_at(gt, step), 7), row_of(herm_at(gt_in, 2 + step), 7), x_down_t_up))
        minus = jnp.where(index_of(0, 3) == 0, 0.0, pltpu.roll(columns, 1, 1))
        for d in (1, 2):
            m = link(d)
            plus = h_add(plus, gram_rows(m))
            minus = minus + shift(h_pack(gram_cols(m)), d, -1)
        herm_at(part, step)[...] = h_pack(plus) - minus
        got.append(send(herm_at(part, step), herm_at(part_in, step), x_down))
        got.append(send(row_of(herm_at(part, step), 0), row_of(herm_at(part_in, 2 + step), 0), t_down))
        return plus[0][0] + plus[0][1] + plus[0][2], got

    def transforms(step, got):
        for copy in got:
            copy.wait_recv()
        first = index_of(0, 3) == 0
        here = herm_at(part, step)[...] - herm_at(gx_in, step)[...] - jnp.where(first, herm_at(gt_in, step)[:, 7:8, :], 0.0)
        low, high = cooling_pair(h_unpack(here))
        next_t = herm_at(part_in, 2 + step)[:, 0:1, :] - herm_at(gx_in, 2 + step)[:, 0:1, :] - herm_at(gt, step)[:, 7:8, :]
        next_t = h_pack(cooling_pair(h_unpack(next_t))[1])
        high_t = h_unpack(shift(h_pack(high), 3, 1, next_t))
        next_x = herm_at(part_in, step)[...] - herm_at(gx, step)[...] - jnp.where(first, herm_at(gt_in, 2 + step)[:, 7:8, :], 0.0)
        high_x = cooling_pair(h_unpack(next_x))[1]
        return low, (high_x, h_shift(high, 1, 1), h_shift(high, 2, 1), high_t)

    def first_links(d):
        m = update(d)
        store(matrix_at(new, d), m)
        return m

    norm, got = exchange(0, first_links)
    norms = [norm]
    low, high = transforms(0, got)

    def second_links(d):
        m = times_h(h_times(low, load(matrix_at(new, d))), high[d])
        store(matrix_at(new, d), m)
        return m

    norm, got = exchange(1, second_links)
    norms.append(norm)
    low, high = transforms(1, got)

    total = None
    for d in range(4):
        m = times_h(h_times(low, load(matrix_at(new, d))), high[d])
        store(matrix_at(out, d), m)
        squares = m[0] * m[0] + m[1] * m[1]
        squares = squares[0] + squares[1] + squares[2]
        squares = squares[0] + squares[1] + squares[2]
        total = squares if total is None else total + squares
    norms.append(total)


    row, lane = index_of(0, 2), index_of(1, 2)
    spread = jnp.zeros(TILE, jnp.float32)
    for at, value in enumerate(norms):
        sums = jnp.sum(value, axis=1, keepdims=True)
        spread = jnp.where(lane == row + ROWS * at, sums, spread)
    mine = jnp.sum(spread, axis=0, keepdims=True)
    norm_row[0:1, :] = mine
    norm_rows[j, 0:1, :] = mine

    def norm_copy(d, at):
        return pltpu.make_async_remote_copy(
            src_ref=norm_row.at[0:1, :],
            dst_ref=norm_rows.at[at, 0:1, :],
            send_sem=norm_send.at[d],
            recv_sem=norm_recv.at[at],
            device_id=(k, group[d]),
            device_id_type=MESH,
        )

    norm_copies = [norm_copy(d, j) for d in range(n_sa - 1)]
    for copy in norm_copies:
        copy.start()
    for copy in started + slab_copies:
        copy.wait_send()
    for d in range(n_sa - 1):
        norm_copy(d, group[d]).wait_recv()
    total = norm_rows[0, 0:1, :]
    for at in range(1, n_sa):
        total = total + norm_rows[at, 0:1, :]
    total = total * (1.0 / (4.0 * n_sa * LANES)) - 3.0
    for at in range(3):
        norm_ref[at : at + 1, :] = total[:, ROWS * at : ROWS * (at + 1)]
    for copy in norm_copies:
        copy.wait_send()


def local(gauge_links, noise_field):
    n_ta, n_sa = lax.axis_size("ta"), lax.axis_size("sa")
    n_in = max(n_sa // 4, 2)
    shape = (4 * MAT,) + TILE
    vmem = lambda *s: pltpu.VMEM(s, jnp.float32)
    dma = lambda n: pltpu.SemaphoreType.DMA((n,))
    cooled, norms = pl.pallas_call(
        functools.partial(kernel, (n_ta, n_sa, n_in)),
        out_shape=(
            pltpu.VMEM(shape, jnp.float32),
            pltpu.VMEM((3, ROWS), jnp.float32),
        ),
        in_specs=[pl.BlockSpec(memory_space=pltpu.HBM)] * 2,
        out_specs=(pl.BlockSpec(memory_space=pltpu.VMEM),) * 2,
        scratch_shapes=[
            vmem(*shape),
            vmem(4, 8, *TILE),
            vmem(*shape),
            vmem(3 * MAT, *TILE),
            vmem(3 * MAT, *TILE),
            vmem(MAT, *TILE),
            vmem(MAT, *TILE),
            vmem(3 * MAT, *TILE),
            vmem(3 * MAT, *TILE),
            vmem(3 * MAT, *TILE),
            vmem(3 * MAT, *TILE),
            vmem(MAT, *TILE),
            vmem(2 * MAT, *TILE),
            vmem(MAT, *TILE),
            vmem(*shape),
            vmem(*shape),
            vmem(2 * HERM, *TILE),
            vmem(4 * HERM, *TILE),
            vmem(2 * HERM, *TILE),
            vmem(4 * HERM, *TILE),
            vmem(2 * HERM, *TILE),
            vmem(4 * HERM, *TILE),
            vmem(*TILE),
            vmem(n_sa, *TILE),
            dma(5),
            dma(22),
            dma(22),
            dma(n_ta - 1),
            dma(n_ta - 1),
            dma(n_sa - 1),
            dma(n_sa),
        ],
        compiler_params=pltpu.CompilerParams(
            collective_id=0, has_side_effects=True, vmem_limit_bytes=VMEM_LIMIT
        ),
        name="langevin_step",
    )(
        pltpu.with_memory_space_constraint(gauge_links.reshape(shape), pltpu.HBM),
        pltpu.with_memory_space_constraint(noise_field.reshape((4, 8) + TILE), pltpu.HBM),
    )
    return cooled.reshape(gauge_links.shape), norms


def solution(mesh):
    placed = (P(None, None, None, None, "sa", "ta", None), P(None, None, "sa", "ta", None))
    return jax.shard_map(
        local,
        mesh=mesh,
        in_specs=placed,
        out_specs=(P(None, None, None, None, "sa", "ta", None), P(None, "ta")),
        check_vma=False,
    )
```

```python
import functools
import math

import jax
import jax.numpy as jnp
from jax import lax
from jax.experimental import pallas as pl
from jax.experimental.pallas import tpu as pltpu
from jax.sharding import PartitionSpec as P

NY = 8
NZ = 16
LANES = NY * NZ
ROWS = 8

COUPLING = 5.6
STEP_SIZE = 0.02
COOL_SIZE = 0.02
FUGACITY = 0.5
ANTI_FUGACITY = 0.02

MESH = pl.DeviceIdType.MESH
VMEM_LIMIT = 32 * 1024 * 1024
TILE = (ROWS, LANES)
MATRIX = (3, 3) + TILE
MAT = 18
HERM = 9


def load(ref):
    return (ref[0:9].reshape(MATRIX), ref[9:18].reshape(MATRIX))


def load_row(ref, row):
    shape = (3, 3, 1, LANES)
    return tuple(ref[9 * c : 9 * c + 9, row : row + 1, :].reshape(shape) for c in range(2))


def store(ref, m):
    ref[0:9] = m[0].reshape((9,) + TILE)
    ref[9:18] = m[1].reshape((9,) + TILE)


def matrix_at(ref, at):
    return ref.at[MAT * at : MAT * (at + 1)]


def herm_at(ref, at):
    return ref.at[HERM * at : HERM * (at + 1)]


def row_of(ref, row):
    return ref.at[:, row : row + 1, :]


def add(a, b):
    return (a[0] + b[0], a[1] + b[1])


def sub(a, b):
    return (a[0] - b[0], a[1] - b[1])


def mm(a, b):
    ar, ai = a
    br, bi = b
    re = im = None
    for k in range(3):
        cr, ci = ar[:, k : k + 1], ai[:, k : k + 1]
        rr, ri = br[k : k + 1], bi[k : k + 1]
        tr = cr * rr - ci * ri
        ti = cr * ri + ci * rr
        re = tr if re is None else re + tr
        im = ti if im is None else im + ti
    return (re, im)


def roll_rows(x, n):
    return jnp.concatenate([x[n:], x[:n]], axis=0)


def roll_cols(x, n):
    return jnp.concatenate([x[:, n:], x[:, :n]], axis=1)


def transposed(x):
    return jnp.stack([x[:, i] for i in range(3)])


def cmul(a, b):
    return (a[0] * b[0] - a[1] * b[1], a[0] * b[1] + a[1] * b[0])


def adj(m):
    one = tuple(roll_rows(x, 1) for x in m)
    two = tuple(roll_rows(x, 2) for x in m)
    plus = cmul(tuple(roll_cols(x, 1) for x in one), tuple(roll_cols(x, 2) for x in two))
    minus = cmul(tuple(roll_cols(x, 2) for x in one), tuple(roll_cols(x, 1) for x in two))
    return (transposed(plus[0] - minus[0]), transposed(plus[1] - minus[1]))


def less_inverse(p):
    return sub(p, adj(p))


def entry(m, i, j):
    return (m[0][i, j], m[1][i, j])


def add_diagonal(x, value):
    rows = []
    for i in range(3):
        parts = [(x[i, i] + value)[None]]
        if i > 0:
            parts.insert(0, x[i, :i])
        if i < 2:
            parts.append(x[i, i + 1 :])
        rows.append(jnp.concatenate(parts, axis=0))
    return jnp.stack(rows)


def inverse(m):
    a = adj(m)
    det = cmul(entry(m, 0, 0), entry(a, 0, 0))
    for j in (1, 2):
        det = add(det, cmul(entry(m, 0, j), entry(a, j, 0)))
    scale = 1.0 / (det[0] * det[0] + det[1] * det[1])
    factor = ((det[0] * scale)[None, None], (-det[1] * scale)[None, None])
    return cmul(a, factor)


def exp_times(y, u):
    square = mm(y, y)
    trace = tuple(x[0, 0] + x[1, 1] + x[2, 2] for x in square)
    det = None
    for j in range(3):
        a, b = (j + 1) % 3, (j + 2) % 3
        minor = sub(
            cmul(entry(y, 1, a), entry(y, 2, b)), cmul(entry(y, 1, b), entry(y, 2, a))
        )
        term = cmul(entry(y, 0, j), minor)
        det = term if det is None else add(det, term)
    beta = ((1.0 + trace[0] * (1.0 / 12.0))[None, None], (trace[1] * (1.0 / 12.0))[None, None])
    linear = cmul(y, beta)
    re = add_diagonal(linear[0] + 0.5 * square[0], 1.0 + det[0] * (1.0 / 6.0))
    im = add_diagonal(linear[1] + 0.5 * square[1], det[1] * (1.0 / 6.0))
    return mm((re, im), u)


def gram_rows(m):
    re, im = m
    diag = re * re + im * im
    a = tuple(jnp.concatenate([x[0:1], x[0:1], x[1:2]], axis=0) for x in m)
    b = tuple(jnp.concatenate([x[1:2], x[2:3], x[2:3]], axis=0) for x in m)
    pr = a[0] * b[0] + a[1] * b[1]
    pi = a[1] * b[0] - a[0] * b[1]
    return tuple(x[:, 0] + x[:, 1] + x[:, 2] for x in (diag, pr, pi))


def gram_cols(m):
    re, im = m
    diag = re * re + im * im
    a = tuple(jnp.concatenate([x[:, 0:1], x[:, 0:1], x[:, 1:2]], axis=1) for x in m)
    b = tuple(jnp.concatenate([x[:, 1:2], x[:, 2:3], x[:, 2:3]], axis=1) for x in m)
    pr = a[0] * b[0] + a[1] * b[1]
    pi = a[0] * b[1] - a[1] * b[0]
    return tuple(x[0] + x[1] + x[2] for x in (diag, pr, pi))


def h_add(a, b):
    return tuple(x + y for x, y in zip(a, b))


def h_sub(a, b):
    return tuple(x - y for x, y in zip(a, b))


def h_pack(h):
    return jnp.concatenate(h, axis=0)


def h_unpack(x):
    return (x[0:3], x[3:6], x[6:9])


def h_offsets(h):
    _, r, i = h
    one = (jnp.stack([r[0], r[2], r[1]]), jnp.stack([i[0], i[2], -i[1]]))
    two = (jnp.stack([r[1], r[0], r[2]]), jnp.stack([i[1], -i[0], -i[2]]))
    return one, two


def h_times(h, m):
    d = h[0][:, None]
    one, two = h_offsets(h)
    re, im = d * m[0], d * m[1]
    for n, off in ((1, one), (2, two)):
        r, i = off[0][:, None], off[1][:, None]
        ur, ui = roll_rows(m[0], n), roll_rows(m[1], n)
        re = re + r * ur - i * ui
        im = im + r * ui + i * ur
    return (re, im)


def times_h(m, h):
    d = h[0][None]
    one, two = h_offsets(h)
    re, im = m[0] * d, m[1] * d
    for n, off in ((1, one), (2, two)):
        r, i = off[0][None], off[1][None]
        ur, ui = roll_cols(m[0], n), roll_cols(m[1], n)
        re = re + ur * r + ui * i
        im = im + ui * r - ur * i
    return (re, im)


def h_full(h):
    d, r, i = h
    zero = jnp.zeros_like(d[0])
    re = jnp.stack(
        [jnp.stack([d[0], r[0], r[1]]), jnp.stack([r[0], d[1], r[2]]), jnp.stack([r[1], r[2], d[2]])]
    )
    im = jnp.stack(
        [jnp.stack([zero, i[0], i[1]]), jnp.stack([-i[0], zero, i[2]]), jnp.stack([-i[1], -i[2], zero])]
    )
    return (re, im)


def h_sandwich(h, s):
    m = times_h(h_times(h, h_full(s)), h)
    return (
        jnp.stack([m[0][0, 0], m[0][1, 1], m[0][2, 2]]),
        jnp.stack([m[0][0, 1], m[0][0, 2], m[0][1, 2]]),
        jnp.stack([m[1][0, 1], m[1][0, 2], m[1][1, 2]]),
    )


def cooling_pair(g):
    third = (g[0][0] + g[0][1] + g[0][2]) * (1.0 / 3.0)
    d = g[0] - third[None]
    p, q, r = ((g[1][n], g[2][n]) for n in range(3))
    norms = g[1] * g[1] + g[2] * g[2]
    np_, nq, nr = norms[0], norms[1], norms[2]
    d0, d1, d2 = d[0], d[1], d[2]
    s0 = d0 * d0 + np_ + nq
    s1 = d1 * d1 + np_ + nr
    s2 = d2 * d2 + nq + nr
    sp = (q[0] * r[0] + q[1] * r[1] - d2 * p[0], q[1] * r[0] - q[0] * r[1] - d2 * p[1])
    prod = cmul(p, r)
    sq = (prod[0] - d1 * q[0], prod[1] - d1 * q[1])
    sr = (p[0] * q[0] + p[1] * q[1] - d0 * r[0], p[0] * q[1] - p[1] * q[0] - d0 * r[1])
    half = 0.5 * (s0 + s1 + s2)
    det = (
        d0 * d1 * d2
        + 2.0 * (prod[0] * q[0] + prod[1] * q[1])
        - d0 * nr
        - d1 * nq
        - d2 * np_
    )
    a = COOL_SIZE
    linear = (a + (a**3 / 6.0) * half)[None]
    constant = ((a**3 / 6.0) * det)[None]
    even = (
        1.0 + (a * a / 2.0) * jnp.stack([s0, s1, s2]),
        (a * a / 2.0) * jnp.stack([sp[0], sq[0], sr[0]]),
        (a * a / 2.0) * jnp.stack([sp[1], sq[1], sr[1]]),
    )
    odd = (linear * d + constant, linear * g[1], linear * g[2])
    return h_sub(even, odd), h_add(even, odd)


def index_of(axis, ndim):
    return lax.broadcasted_iota(jnp.int32, (1,) * (ndim - 2) + TILE, ndim - 2 + axis)


def shift(x, direction, sign, halo=None):
    n = x.ndim
    if direction == 1:
        return pltpu.roll(x, LANES - NZ if sign > 0 else NZ, n - 1)
    if direction == 2:
        z = index_of(1, n) % NZ
        if sign > 0:
            return jnp.where(
                z == NZ - 1, pltpu.roll(x, NZ - 1, n - 1), pltpu.roll(x, LANES - 1, n - 1)
            )
        return jnp.where(z == 0, pltpu.roll(x, LANES - NZ + 1, n - 1), pltpu.roll(x, 1, n - 1))
    t = index_of(0, n)
    if sign > 0:
        return jnp.where(t == ROWS - 1, halo, pltpu.roll(x, ROWS - 1, n - 2))
    return jnp.where(t == 0, halo, pltpu.roll(x, 1, n - 2))


def m_shift(m, direction, sign, halo=(None, None)):
    return (shift(m[0], direction, sign, halo[0]), shift(m[1], direction, sign, halo[1]))


def h_shift(h, direction, sign, halo=None):
    return h_unpack(shift(h_pack(h), direction, sign, halo))


def unit_where(m, mask):
    one = jnp.where(mask, 1.0, 0.0)
    re = jnp.where(mask, 0.0, m[0])
    im = jnp.where(mask, 0.0, m[1])
    return (add_diagonal(re, one[0, 0]), im)


def time_scan(u, reverse):
    t = index_of(0, 4)
    for step in (1, 2, 4):
        if reverse:
            other = tuple(pltpu.roll(x, ROWS - step, 2) for x in u)
            u = mm(u, unit_where(other, t >= ROWS - step))
        else:
            other = tuple(pltpu.roll(x, step, 2) for x in u)
            u = mm(unit_where(other, t < step), u)
    return u


def far_first(n_out, n_in):
    steps = [(a, b) for a in range(n_out) for b in range(n_in) if a or b]
    return sorted(steps, key=lambda s: -(min(s[0], n_out - s[0]) + min(s[1], n_in - s[1])))


def kernel(
    sizes,
    u_hbm,
    noise_hbm,
    out,
    norm_ref,
    u,
    noise,
    inv,
    ahead_x,
    ahead_t,
    ahead_xt,
    behind_xt,
    qx,
    qx_in,
    qt,
    qt_in,
    slab,
    slabs,
    prefix,
    middles,
    acc,
    new,
    gx,
    gx_in,
    gt,
    gt_in,
    part,
    part_in,
    norm_row,
    norm_rows,
    local_sem,
    send_sem,
    recv_sem,
    slab_send,
    slab_recv,
    norm_send,
    norm_recv,
):
    n_ta, n_sa, n_in = sizes
    n_out = n_sa // n_in
    k, j = lax.axis_index("ta"), lax.axis_index("sa")
    j_out, j_in = j // n_in, j % n_in
    k_up, k_down = lax.rem(k + 1, n_ta), lax.rem(k + n_ta - 1, n_ta)
    j_up, j_down = lax.rem(j + 1, n_sa), lax.rem(j + n_sa - 1, n_sa)
    t_up, t_down, x_up, x_down = (k_up, j), (k_down, j), (k, j_up), (k, j_down)
    x_up_t_down, x_down_t_up = (k_down, j_up), (k_up, j_down)
    around = [lax.rem(k + n_ta - d, n_ta) for d in range(1, n_ta)]
    group = [
        lax.rem(j_out + a, n_out) * n_in + lax.rem(j_in + b, n_in)
        for a, b in far_first(n_out, n_in)
    ]

    barrier = pltpu.get_barrier_semaphore()
    partners = [
        (min(a, n_out - a) + min(b, n_in - b), (k, at))
        for (a, b), at in zip(far_first(n_out, n_in), group)
    ]
    partners += [(8 + min(d, n_ta - d), (at, j)) for d, at in enumerate(around, 1)]
    partners += [(2.5, x_up_t_down), (2.5, x_down_t_up)]
    partners = [device for _, device in sorted(partners, key=lambda p: -p[0])]
    for device in partners:
        pl.semaphore_signal(barrier, inc=1, device_id=device, device_id_type=MESH)

    loads = [pltpu.make_async_copy(matrix_at(u_hbm, d), matrix_at(u, d), local_sem.at[d]) for d in range(4)]
    loads.append(pltpu.make_async_copy(noise_hbm, noise, local_sem.at[4]))
    for copy in loads:
        copy.start()

    started = []

    def send(src, dst, device):
        at = len(started)
        copy = pltpu.make_async_remote_copy(
            src_ref=src,
            dst_ref=dst,
            send_sem=send_sem.at[at],
            recv_sem=recv_sem.at[at],
            device_id=device,
            device_id_type=MESH,
        )
        copy.start()
        started.append(copy)
        return copy

    def accumulate(d, term, sign):
        now = load(matrix_at(acc, d))
        store(matrix_at(acc, d), add(now, term) if sign > 0 else sub(now, term))


    links = [matrix_at(u, d) for d in range(4)]
    invs = [matrix_at(inv, d) for d in range(4)]
    t_of = index_of(0, 4)
    for d in range(4):
        loads[d].wait()
        store(invs[d], adj(load(links[d])))

    for nu in (1, 2):
        middle = mm(load(invs[nu]), load(links[0]))
        store(matrix_at(middles, nu - 1), middle)
        store(matrix_at(qx, nu - 1), mm(m_shift(load(invs[0]), nu, 1), middle))
    middle = mm(load(invs[3]), load(links[0]))
    store(matrix_at(qt, 0), middle)
    raised = tuple(pltpu.roll(x, ROWS - 1, 2) for x in load(invs[0]))
    whole = mm(raised, middle)
    store(matrix_at(qx, 2), tuple(jnp.where(t_of == ROWS - 1, b, a) for a, b in zip(whole, middle)))

    for nu in (1, 2):
        middle = mm(load(invs[3]), load(links[nu]))
        store(matrix_at(middles, 1 + nu), middle)
        store(matrix_at(qt, nu), mm(middle, m_shift(load(links[3]), nu, 1)))

    store(slab, time_scan(load(links[3]), True))
    scan = time_scan(load(links[3]), False)
    store(prefix, unit_where(tuple(pltpu.roll(x, 1, 2) for x in scan), t_of == 0))

    u_1, u_2 = load(links[1]), load(links[2])
    n_12 = mm(m_shift(u_2, 1, 1), m_shift(load(invs[1]), 2, 1))
    m_12 = mm(load(invs[2]), u_1)
    a_12 = less_inverse(mm(u_1, mm(n_12, load(invs[2]))))
    store(matrix_at(acc, 1), sub(a_12, m_shift(less_inverse(mm(m_12, n_12)), 2, -1)))
    store(matrix_at(acc, 2), sub(m_shift(less_inverse(mm(n_12, m_12)), 1, -1), a_12))


    pl.semaphore_wait(barrier, len(partners))

    got_ux, got_qx = {}, {}
    for nu in (3, 1, 2):
        got_ux[nu] = send(links[nu], matrix_at(ahead_x, nu - 1), x_down)
        got_qx[nu] = send(matrix_at(qx, nu - 1), matrix_at(qx_in, nu - 1), x_up)
    got_ut = send(inv.at[0 : 3 * MAT, 0:1, :], row_of(ahead_t, 0), t_down)
    got_qt = send(row_of(qt, 7), row_of(qt_in, 7), t_up)
    slab_copies = []
    far_order = sorted(range(1, n_ta), key=lambda d: -min(d, n_ta - d))
    for d in far_order:
        at = d - 1
        row = at // 2
        copy = pltpu.make_async_remote_copy(
            src_ref=row_of(slab, 0),
            dst_ref=row_of(matrix_at(slabs, at % 2), row),
            send_sem=slab_send.at[at],
            recv_sem=slab_recv.at[at],
            device_id=(around[at], j),
            device_id_type=MESH,
        )
        copy.start()
        slab_copies.append(copy)
    got_inv_xt = send(row_of(invs[0], 0), row_of(ahead_xt, 0), x_up_t_down)
    got_u_xt = send(row_of(links[3], 7), row_of(behind_xt, 7), x_down_t_up)

    got_ut.wait_recv()

    def inv_ahead(nu):
        return load_row(matrix_at(ahead_t, nu), 0)

    got_qt.wait_recv()

    def behind_t(nu):
        return load_row(matrix_at(qt_in, nu), 7)

    for nu in (1, 2):
        n_nt = mm(m_shift(load(links[3]), nu, 1), m_shift(load(invs[nu]), 3, 1, inv_ahead(nu)))
        a_nt = less_inverse(mm(load(links[nu]), mm(n_nt, load(invs[3]))))
        m_nt = load(matrix_at(middles, 1 + nu))
        lower = mm(m_shift(load(matrix_at(qt, nu)), 3, -1, behind_t(nu)), load(invs[nu]))
        accumulate(nu, sub(a_nt, less_inverse(lower)), 1)
        to_t = sub(m_shift(less_inverse(mm(n_nt, m_nt)), nu, -1), a_nt)
        if nu == 1:
            store(matrix_at(acc, 3), to_t)
        else:
            accumulate(3, to_t, 1)

    for copy in slab_copies:
        copy.wait_recv()
    slot = 2 * t_of
    even, odd = load(matrix_at(slabs, 0)), load(matrix_at(slabs, 1))
    if n_ta - 1 < 2 * ROWS - 1:
        even = unit_where(even, slot >= n_ta - 1)
    odd = unit_where(odd, slot + 1 >= n_ta - 1)
    others = mm(even, odd)
    for step in (1, 2, 4):
        others = mm(others, tuple(pltpu.roll(x, ROWS - step, 2) for x in others))
    others = tuple(jnp.broadcast_to(x[:, :, 0:1, :], x.shape) for x in others)
    line = mm(mm(load(slab), others), load(prefix))
    back = adj(line)
    former = (add_diagonal(FUGACITY * line[0], 1.0), FUGACITY * line[1])
    latter = (add_diagonal(ANTI_FUGACITY * back[0], 1.0), ANTI_FUGACITY * back[1])
    drift = sub(inverse(latter), inverse(former))
    weight = 4.0 * 3.0 / COUPLING
    accumulate(3, (weight * drift[0], weight * drift[1]), 1)

    for nu in (3, 1, 2):
        got_ux[nu].wait_recv()
        halo = inv_ahead(0) if nu == 3 else (None, None)
        n_xn = mm(load(matrix_at(ahead_x, nu - 1)), m_shift(load(invs[0]), nu, 1, halo))
        a_xn = less_inverse(mm(load(links[0]), mm(n_xn, load(invs[nu]))))
        if nu == 3:
            got_u_xt.wait_recv()
            ahead = load_row(behind_xt, 7)
            corner = mm(load(matrix_at(qt, 0)), load(matrix_at(ahead_x, 2)))
            corner = m_shift(corner, 3, -1, mm(behind_t(0), ahead))
            store(matrix_at(acc, 0), sub(a_xn, less_inverse(mm(corner, load(invs[0])))))
        else:
            m_xn = load(matrix_at(middles, nu - 1))
            lower = m_shift(less_inverse(mm(m_xn, n_xn)), nu, -1)
            accumulate(0, sub(a_xn, lower), 1)
        got_qx[nu].wait_recv()
        corner = load(matrix_at(qx_in, nu - 1))
        if nu == 3:
            got_inv_xt.wait_recv()
            ahead = load_row(ahead_xt, 0)
            fixed = mm(ahead, corner)
            corner = tuple(jnp.where(t_of == ROWS - 1, b, a) for a, b in zip(corner, fixed))
        accumulate(nu, sub(less_inverse(mm(load(links[nu]), corner)), a_xn), 1)

    loads[4].wait()
    c = math.sqrt(STEP_SIZE)

    def update(d):
        x = load(matrix_at(acc, d))
        w = -STEP_SIZE * COUPLING / 3.0
        mean_r = (x[0][0, 0] + x[0][1, 1] + x[0][2, 2]) * (1.0 / 3.0)
        mean_i = (x[1][0, 0] + x[1][1, 1] + x[1][2, 2]) * (1.0 / 3.0)
        n = [c * noise[d, a] for a in range(8)]
        n7 = n[7] * (1.0 / math.sqrt(3.0))
        real = {(0, 1): n[1], (0, 2): n[4], (1, 2): n[6]}
        imag = {(0, 1): n[0], (0, 2): n[3], (1, 2): n[5]}
        diag = (n[2] + n7, n7 - n[2], -2.0 * n7)
        yr, yi = [], []
        for a in range(3):
            row_r, row_i = [], []
            for b in range(3):
                if a == b:
                    row_r.append(w * (x[0][a, b] - mean_r))
                    row_i.append(w * (x[1][a, b] - mean_i) + diag[a])
                elif a < b:
                    row_r.append(w * x[0][a, b] + real[a, b])
                    row_i.append(w * x[1][a, b] + imag[a, b])
                else:
                    row_r.append(w * x[0][a, b] - real[b, a])
                    row_i.append(w * x[1][a, b] + imag[b, a])
            yr.append(jnp.stack(row_r))
            yi.append(jnp.stack(row_i))
        return exp_times((jnp.stack(yr), jnp.stack(yi)), load(links[d]))


    def exchange(step, link, order):
        plus = minus = None
        got = {}
        for d in order:
            m = link(d)
            rows, columns = gram_rows(m), h_pack(gram_cols(m))
            plus = rows if plus is None else h_add(plus, rows)
            if d == 0:
                mine = herm_at(gx, step)
                mine[...] = columns
                got["x"] = send(mine, herm_at(gx_in, step), x_up)
                there = row_of(herm_at(gx_in, 2 + step), 0)
                got["x ahead"] = send(row_of(mine, 0), there, x_up_t_down)
                continue
            if d == 3:
                mine = herm_at(gt, step)
                mine[...] = columns
                mine = row_of(mine, 7)
                got["t"] = send(mine, row_of(herm_at(gt_in, step), 7), t_up)
                got["t ahead"] = send(mine, row_of(herm_at(gt_in, 2 + step), 7), x_down_t_up)
                lagged = jnp.where(index_of(0, 3) == 0, 0.0, pltpu.roll(columns, 1, 1))
            else:
                lagged = shift(columns, d, -1)
            minus = lagged if minus is None else minus + lagged
        mine = herm_at(part, step)
        mine[...] = h_pack(plus) - minus
        got["part x"] = send(mine, herm_at(part_in, step), x_down)
        got["part t"] = send(row_of(mine, 0), row_of(herm_at(part_in, 2 + step), 0), t_down)
        return plus[0][0] + plus[0][1] + plus[0][2], got

    def transforms(step, got):
        first = index_of(0, 3) == 0
        got["t"].wait_recv()
        got["x"].wait_recv()
        lag = jnp.where(first, herm_at(gt_in, step)[:, 7:8, :], 0.0)
        here = herm_at(part, step)[...] - herm_at(gx_in, step)[...] - lag
        low, high = cooling_pair(h_unpack(here))

        def ahead(d):
            if d == 3:
                got["part t"].wait_recv()
                got["x ahead"].wait_recv()
                g = herm_at(part_in, 2 + step)[:, 0:1, :] - herm_at(gx_in, 2 + step)[:, 0:1, :]
                g = g - herm_at(gt, step)[:, 7:8, :]
                halo = h_pack(cooling_pair(h_unpack(g))[1])
                return h_unpack(shift(h_pack(high), 3, 1, halo))
            if d == 0:
                got["t ahead"].wait_recv()
                got["part x"].wait_recv()
                g = herm_at(part_in, step)[...] - herm_at(gx, step)[...]
                g = g - jnp.where(first, herm_at(gt_in, 2 + step)[:, 7:8, :], 0.0)
                return cooling_pair(h_unpack(g))[1]
            return h_shift(high, d, 1)

        return low, ahead

    def lane_sums(value):
        return jnp.sum(value, axis=1, keepdims=True)

    def first_links(d):
        m = update(d)
        store(matrix_at(new, d), m)
        return m

    norm, got = exchange(0, first_links, (0, 3, 1, 2))
    norms = [lane_sums(norm)]
    low, ahead = transforms(0, got)

    def cooled_link(d):
        m = h_times(low, load(matrix_at(new, d)))
        return times_h(m, ahead(d))

    def second_links(d):
        m = cooled_link(d)
        store(matrix_at(new, d), m)
        return m

    norm, got = exchange(1, second_links, (1, 2, 3, 0))
    norms.append(lane_sums(norm))
    low, ahead = transforms(1, got)

    total = None
    for d in (1, 2, 3, 0):
        m = cooled_link(d)
        store(matrix_at(out, d), m)
        squares = m[0] * m[0] + m[1] * m[1]
        squares = squares[0] + squares[1] + squares[2]
        squares = squares[0] + squares[1] + squares[2]
        total = squares if total is None else total + squares
    norms.append(lane_sums(total))


    row, lane = index_of(0, 2), index_of(1, 2)
    spread = jnp.zeros(TILE, jnp.float32)
    for at, sums in enumerate(norms):
        spread = jnp.where(lane == row + ROWS * at, sums, spread)
    mine = jnp.sum(spread, axis=0, keepdims=True)
    norm_row[0:1, :] = mine
    norm_rows[j, 0:1, :] = mine

    def norm_copy(d, at):
        return pltpu.make_async_remote_copy(
            src_ref=norm_row.at[0:1, :],
            dst_ref=norm_rows.at[at, 0:1, :],
            send_sem=norm_send.at[d],
            recv_sem=norm_recv.at[at],
            device_id=(k, group[d]),
            device_id_type=MESH,
        )

    norm_copies = [norm_copy(d, j) for d in range(n_sa - 1)]
    for copy in norm_copies:
        copy.start()
    for copy in started + slab_copies:
        copy.wait_send()
    for d in range(n_sa - 1):
        norm_copy(d, group[d]).wait_recv()
    total = norm_rows[0, 0:1, :]
    for at in range(1, n_sa):
        total = total + norm_rows[at, 0:1, :]
    total = total * (1.0 / (4.0 * n_sa * LANES)) - 3.0
    for at in range(3):
        norm_ref[at : at + 1, :] = total[:, ROWS * at : ROWS * (at + 1)]
    for copy in norm_copies:
        copy.wait_send()


def finish(links, norms, links_out, norms_out, sem):
    copies = (
        pltpu.make_async_copy(links, links_out, sem.at[0]),
        pltpu.make_async_copy(norms, norms_out, sem.at[1]),
    )
    for copy in copies:
        copy.start()
    for copy in copies:
        copy.wait()


def local(gauge_links, noise_field):
    n_ta, n_sa = lax.axis_size("ta"), lax.axis_size("sa")
    n_in = max(n_sa // 4, 2)
    shape = (4 * MAT,) + TILE
    vmem = lambda *s: pltpu.VMEM(s, jnp.float32)
    dma = lambda n: pltpu.SemaphoreType.DMA((n,))
    cooled, norms = pl.pallas_call(
        functools.partial(kernel, (n_ta, n_sa, n_in)),
        out_shape=(
            pltpu.VMEM(shape, jnp.float32),
            pltpu.VMEM((3, ROWS), jnp.float32),
        ),
        in_specs=[pl.BlockSpec(memory_space=pltpu.HBM)] * 2,
        out_specs=(pl.BlockSpec(memory_space=pltpu.VMEM),) * 2,
        scratch_shapes=[
            vmem(*shape),
            vmem(4, 8, *TILE),
            vmem(*shape),
            vmem(3 * MAT, *TILE),
            vmem(3 * MAT, *TILE),
            vmem(MAT, *TILE),
            vmem(MAT, *TILE),
            vmem(3 * MAT, *TILE),
            vmem(3 * MAT, *TILE),
            vmem(3 * MAT, *TILE),
            vmem(3 * MAT, *TILE),
            vmem(MAT, *TILE),
            vmem(2 * MAT, *TILE),
            vmem(MAT, *TILE),
            vmem(4 * MAT, *TILE),
            vmem(*shape),
            vmem(*shape),
            vmem(2 * HERM, *TILE),
            vmem(4 * HERM, *TILE),
            vmem(2 * HERM, *TILE),
            vmem(4 * HERM, *TILE),
            vmem(2 * HERM, *TILE),
            vmem(4 * HERM, *TILE),
            vmem(*TILE),
            vmem(n_sa, *TILE),
            dma(5),
            dma(22),
            dma(22),
            dma(n_ta - 1),
            dma(n_ta - 1),
            dma(n_sa - 1),
            dma(n_sa),
        ],
        compiler_params=pltpu.CompilerParams(
            collective_id=0, has_side_effects=True, vmem_limit_bytes=VMEM_LIMIT
        ),
        name="langevin_step",
    )(
        pltpu.with_memory_space_constraint(gauge_links.reshape(shape), pltpu.HBM),
        pltpu.with_memory_space_constraint(noise_field.reshape((4, 8) + TILE), pltpu.HBM),
    )
    cooled, norms = pl.pallas_call(
        finish,
        out_shape=(
            jax.ShapeDtypeStruct(shape, jnp.float32),
            jax.ShapeDtypeStruct((3, ROWS), jnp.float32),
        ),
        in_specs=[pl.BlockSpec(memory_space=pltpu.VMEM)] * 2,
        out_specs=(pl.BlockSpec(memory_space=pltpu.HBM),) * 2,
        scratch_shapes=[dma(2)],
        compiler_params=pltpu.CompilerParams(vmem_limit_bytes=VMEM_LIMIT),
        name="write_out",
    )(cooled, norms)
    return cooled.reshape(gauge_links.shape), norms


def solution(mesh):
    placed = (P(None, None, None, None, "sa", "ta", None), P(None, None, "sa", "ta", None))
    return jax.shard_map(
        local,
        mesh=mesh,
        in_specs=placed,
        out_specs=(P(None, None, None, None, "sa", "ta", None), P(None, "ta")),
        check_vma=False,
    )
```

```python
import functools
import math

import jax
import jax.numpy as jnp
from jax import lax
from jax.experimental import pallas as pl
from jax.experimental.pallas import tpu as pltpu
from jax.sharding import PartitionSpec as P

NY = 8
NZ = 16
LANES = NY * NZ
ROWS = 8

COUPLING = 5.6
STEP_SIZE = 0.02
COOL_SIZE = 0.02
FUGACITY = 0.5
ANTI_FUGACITY = 0.02

MESH = pl.DeviceIdType.MESH
VMEM_LIMIT = 32 * 1024 * 1024
TILE = (ROWS, LANES)
MATRIX = (3, 3) + TILE
MAT = 18
HERM = 9


def load(ref):
    return (ref[0:9].reshape(MATRIX), ref[9:18].reshape(MATRIX))


def load_row(ref, row):
    shape = (3, 3, 1, LANES)
    return tuple(ref[9 * c : 9 * c + 9, row : row + 1, :].reshape(shape) for c in range(2))


def store(ref, m):
    ref[0:9] = m[0].reshape((9,) + TILE)
    ref[9:18] = m[1].reshape((9,) + TILE)


def matrix_at(ref, at):
    return ref.at[MAT * at : MAT * (at + 1)]


def herm_at(ref, at):
    return ref.at[HERM * at : HERM * (at + 1)]


def row_of(ref, row):
    return ref.at[:, row : row + 1, :]


def add(a, b):
    return (a[0] + b[0], a[1] + b[1])


def sub(a, b):
    return (a[0] - b[0], a[1] - b[1])


def mm(a, b):
    ar, ai = a
    br, bi = b
    re = im = None
    for k in range(3):
        cr, ci = ar[:, k : k + 1], ai[:, k : k + 1]
        rr, ri = br[k : k + 1], bi[k : k + 1]
        tr = cr * rr - ci * ri
        ti = cr * ri + ci * rr
        re = tr if re is None else re + tr
        im = ti if im is None else im + ti
    return (re, im)


def roll_rows(x, n):
    return jnp.concatenate([x[n:], x[:n]], axis=0)


def roll_cols(x, n):
    return jnp.concatenate([x[:, n:], x[:, :n]], axis=1)


def transposed(x):
    return jnp.stack([x[:, i] for i in range(3)])


def cmul(a, b):
    return (a[0] * b[0] - a[1] * b[1], a[0] * b[1] + a[1] * b[0])


def adj(m):
    one = tuple(roll_rows(x, 1) for x in m)
    two = tuple(roll_rows(x, 2) for x in m)
    plus = cmul(tuple(roll_cols(x, 1) for x in one), tuple(roll_cols(x, 2) for x in two))
    minus = cmul(tuple(roll_cols(x, 2) for x in one), tuple(roll_cols(x, 1) for x in two))
    return (transposed(plus[0] - minus[0]), transposed(plus[1] - minus[1]))


def less_inverse(p):
    return sub(p, adj(p))


def entry(m, i, j):
    return (m[0][i, j], m[1][i, j])


def add_diagonal(x, value):
    rows = []
    for i in range(3):
        parts = [(x[i, i] + value)[None]]
        if i > 0:
            parts.insert(0, x[i, :i])
        if i < 2:
            parts.append(x[i, i + 1 :])
        rows.append(jnp.concatenate(parts, axis=0))
    return jnp.stack(rows)


def inverse(m):
    a = adj(m)
    det = cmul(entry(m, 0, 0), entry(a, 0, 0))
    for j in (1, 2):
        det = add(det, cmul(entry(m, 0, j), entry(a, j, 0)))
    scale = 1.0 / (det[0] * det[0] + det[1] * det[1])
    factor = ((det[0] * scale)[None, None], (-det[1] * scale)[None, None])
    return cmul(a, factor)


def exp_times(y, u):
    square = mm(y, y)
    trace = tuple(x[0, 0] + x[1, 1] + x[2, 2] for x in square)
    det = None
    for j in range(3):
        a, b = (j + 1) % 3, (j + 2) % 3
        minor = sub(
            cmul(entry(y, 1, a), entry(y, 2, b)), cmul(entry(y, 1, b), entry(y, 2, a))
        )
        term = cmul(entry(y, 0, j), minor)
        det = term if det is None else add(det, term)
    beta = ((1.0 + trace[0] * (1.0 / 12.0))[None, None], (trace[1] * (1.0 / 12.0))[None, None])
    linear = cmul(y, beta)
    re = add_diagonal(linear[0] + 0.5 * square[0], 1.0 + det[0] * (1.0 / 6.0))
    im = add_diagonal(linear[1] + 0.5 * square[1], det[1] * (1.0 / 6.0))
    return mm((re, im), u)


def gram_rows(m):
    re, im = m
    diag = re * re + im * im
    a = tuple(jnp.concatenate([x[0:1], x[0:1], x[1:2]], axis=0) for x in m)
    b = tuple(jnp.concatenate([x[1:2], x[2:3], x[2:3]], axis=0) for x in m)
    pr = a[0] * b[0] + a[1] * b[1]
    pi = a[1] * b[0] - a[0] * b[1]
    return tuple(x[:, 0] + x[:, 1] + x[:, 2] for x in (diag, pr, pi))


def gram_cols(m):
    re, im = m
    diag = re * re + im * im
    a = tuple(jnp.concatenate([x[:, 0:1], x[:, 0:1], x[:, 1:2]], axis=1) for x in m)
    b = tuple(jnp.concatenate([x[:, 1:2], x[:, 2:3], x[:, 2:3]], axis=1) for x in m)
    pr = a[0] * b[0] + a[1] * b[1]
    pi = a[0] * b[1] - a[1] * b[0]
    return tuple(x[0] + x[1] + x[2] for x in (diag, pr, pi))


def h_add(a, b):
    return tuple(x + y for x, y in zip(a, b))


def h_sub(a, b):
    return tuple(x - y for x, y in zip(a, b))


def h_pack(h):
    return jnp.concatenate(h, axis=0)


def h_unpack(x):
    return (x[0:3], x[3:6], x[6:9])


def h_offsets(h):
    _, r, i = h
    one = (jnp.stack([r[0], r[2], r[1]]), jnp.stack([i[0], i[2], -i[1]]))
    two = (jnp.stack([r[1], r[0], r[2]]), jnp.stack([i[1], -i[0], -i[2]]))
    return one, two


def h_times(h, m):
    d = h[0][:, None]
    one, two = h_offsets(h)
    re, im = d * m[0], d * m[1]
    for n, off in ((1, one), (2, two)):
        r, i = off[0][:, None], off[1][:, None]
        ur, ui = roll_rows(m[0], n), roll_rows(m[1], n)
        re = re + r * ur - i * ui
        im = im + r * ui + i * ur
    return (re, im)


def times_h(m, h):
    d = h[0][None]
    one, two = h_offsets(h)
    re, im = m[0] * d, m[1] * d
    for n, off in ((1, one), (2, two)):
        r, i = off[0][None], off[1][None]
        ur, ui = roll_cols(m[0], n), roll_cols(m[1], n)
        re = re + ur * r + ui * i
        im = im + ui * r - ur * i
    return (re, im)


def h_full(h):
    d, r, i = h
    zero = jnp.zeros_like(d[0])
    re = jnp.stack(
        [jnp.stack([d[0], r[0], r[1]]), jnp.stack([r[0], d[1], r[2]]), jnp.stack([r[1], r[2], d[2]])]
    )
    im = jnp.stack(
        [jnp.stack([zero, i[0], i[1]]), jnp.stack([-i[0], zero, i[2]]), jnp.stack([-i[1], -i[2], zero])]
    )
    return (re, im)


def h_sandwich(h, s):
    m = times_h(h_times(h, h_full(s)), h)
    return (
        jnp.stack([m[0][0, 0], m[0][1, 1], m[0][2, 2]]),
        jnp.stack([m[0][0, 1], m[0][0, 2], m[0][1, 2]]),
        jnp.stack([m[1][0, 1], m[1][0, 2], m[1][1, 2]]),
    )


def cooling_pair(g):
    third = (g[0][0] + g[0][1] + g[0][2]) * (1.0 / 3.0)
    d = g[0] - third[None]
    p, q, r = ((g[1][n], g[2][n]) for n in range(3))
    norms = g[1] * g[1] + g[2] * g[2]
    np_, nq, nr = norms[0], norms[1], norms[2]
    d0, d1, d2 = d[0], d[1], d[2]
    s0 = d0 * d0 + np_ + nq
    s1 = d1 * d1 + np_ + nr
    s2 = d2 * d2 + nq + nr
    sp = (q[0] * r[0] + q[1] * r[1] - d2 * p[0], q[1] * r[0] - q[0] * r[1] - d2 * p[1])
    prod = cmul(p, r)
    sq = (prod[0] - d1 * q[0], prod[1] - d1 * q[1])
    sr = (p[0] * q[0] + p[1] * q[1] - d0 * r[0], p[0] * q[1] - p[1] * q[0] - d0 * r[1])
    half = 0.5 * (s0 + s1 + s2)
    det = (
        d0 * d1 * d2
        + 2.0 * (prod[0] * q[0] + prod[1] * q[1])
        - d0 * nr
        - d1 * nq
        - d2 * np_
    )
    a = COOL_SIZE
    linear = (a + (a**3 / 6.0) * half)[None]
    constant = ((a**3 / 6.0) * det)[None]
    even = (
        1.0 + (a * a / 2.0) * jnp.stack([s0, s1, s2]),
        (a * a / 2.0) * jnp.stack([sp[0], sq[0], sr[0]]),
        (a * a / 2.0) * jnp.stack([sp[1], sq[1], sr[1]]),
    )
    odd = (linear * d + constant, linear * g[1], linear * g[2])
    return h_sub(even, odd), h_add(even, odd)


def index_of(axis, ndim):
    return lax.broadcasted_iota(jnp.int32, (1,) * (ndim - 2) + TILE, ndim - 2 + axis)


def shift(x, direction, sign, halo=None):
    n = x.ndim
    if direction == 1:
        return pltpu.roll(x, LANES - NZ if sign > 0 else NZ, n - 1)
    if direction == 2:
        z = index_of(1, n) % NZ
        if sign > 0:
            return jnp.where(
                z == NZ - 1, pltpu.roll(x, NZ - 1, n - 1), pltpu.roll(x, LANES - 1, n - 1)
            )
        return jnp.where(z == 0, pltpu.roll(x, LANES - NZ + 1, n - 1), pltpu.roll(x, 1, n - 1))
    t = index_of(0, n)
    if sign > 0:
        return jnp.where(t == ROWS - 1, halo, pltpu.roll(x, ROWS - 1, n - 2))
    return jnp.where(t == 0, halo, pltpu.roll(x, 1, n - 2))


def m_shift(m, direction, sign, halo=(None, None)):
    return (shift(m[0], direction, sign, halo[0]), shift(m[1], direction, sign, halo[1]))


def h_shift(h, direction, sign, halo=None):
    return h_unpack(shift(h_pack(h), direction, sign, halo))


def unit_where(m, mask):
    one = jnp.where(mask, 1.0, 0.0)
    re = jnp.where(mask, 0.0, m[0])
    im = jnp.where(mask, 0.0, m[1])
    return (add_diagonal(re, one[0, 0]), im)


def time_scan(u, reverse):
    t = index_of(0, 4)
    for step in (1, 2, 4):
        if reverse:
            other = tuple(pltpu.roll(x, ROWS - step, 2) for x in u)
            u = mm(u, unit_where(other, t >= ROWS - step))
        else:
            other = tuple(pltpu.roll(x, step, 2) for x in u)
            u = mm(unit_where(other, t < step), u)
    return u


def far_first(n_out, n_in):
    steps = [(a, b) for a in range(n_out) for b in range(n_in) if a or b]
    return sorted(steps, key=lambda s: -(min(s[0], n_out - s[0]) + min(s[1], n_in - s[1])))


def kernel(
    sizes,
    u_hbm,
    noise_hbm,
    out,
    norm_ref,
    u,
    noise,
    inv,
    ahead_x,
    ahead_t,
    ahead_xt,
    behind_xt,
    qx,
    qx_in,
    qt,
    qt_in,
    slab,
    slabs,
    prefix,
    middles,
    acc,
    new,
    gx,
    gx_in,
    gt,
    gt_in,
    part,
    part_in,
    norm_row,
    norm_rows,
    local_sem,
    send_sem,
    recv_sem,
    slab_send,
    slab_recv,
    norm_send,
    norm_recv,
):
    n_ta, n_sa, n_in = sizes
    n_out = n_sa // n_in
    k, j = lax.axis_index("ta"), lax.axis_index("sa")
    j_out, j_in = j // n_in, j % n_in
    k_up, k_down = lax.rem(k + 1, n_ta), lax.rem(k + n_ta - 1, n_ta)
    j_up, j_down = lax.rem(j + 1, n_sa), lax.rem(j + n_sa - 1, n_sa)
    t_up, t_down, x_up, x_down = (k_up, j), (k_down, j), (k, j_up), (k, j_down)
    x_up_t_down, x_down_t_up = (k_down, j_up), (k_up, j_down)
    around = [lax.rem(k + n_ta - d, n_ta) for d in range(1, n_ta)]
    group = [
        lax.rem(j_out + a, n_out) * n_in + lax.rem(j_in + b, n_in)
        for a, b in far_first(n_out, n_in)
    ]

    barrier = pltpu.get_barrier_semaphore()
    partners = [
        (min(a, n_out - a) + min(b, n_in - b), (k, at))
        for (a, b), at in zip(far_first(n_out, n_in), group)
    ]
    partners += [(8 + min(d, n_ta - d), (at, j)) for d, at in enumerate(around, 1)]
    partners += [(2.5, x_up_t_down), (2.5, x_down_t_up)]
    partners = [device for _, device in sorted(partners, key=lambda p: -p[0])]
    def greet(devices):
        for device in devices:
            pl.semaphore_signal(barrier, inc=1, device_id=device, device_id_type=MESH)

    greet(partners[: n_ta - 1])
    loads = [pltpu.make_async_copy(matrix_at(u_hbm, d), matrix_at(u, d), local_sem.at[d]) for d in range(4)]
    loads.append(pltpu.make_async_copy(noise_hbm, noise, local_sem.at[4]))
    for copy in loads:
        copy.start()
    greet(partners[n_ta - 1 :])

    started = []

    def send(src, dst, device):
        at = len(started)
        copy = pltpu.make_async_remote_copy(
            src_ref=src,
            dst_ref=dst,
            send_sem=send_sem.at[at],
            recv_sem=recv_sem.at[at],
            device_id=device,
            device_id_type=MESH,
        )
        copy.start()
        started.append(copy)
        return copy

    def accumulate(d, term, sign):
        now = load(matrix_at(acc, d))
        store(matrix_at(acc, d), add(now, term) if sign > 0 else sub(now, term))


    links = [matrix_at(u, d) for d in range(4)]
    invs = [matrix_at(inv, d) for d in range(4)]
    t_of = index_of(0, 4)
    for d in range(4):
        loads[d].wait()
        store(invs[d], adj(load(links[d])))

    for nu in (1, 2):
        middle = mm(load(invs[nu]), load(links[0]))
        store(matrix_at(middles, nu - 1), middle)
        store(matrix_at(qx, nu - 1), mm(m_shift(load(invs[0]), nu, 1), middle))
    middle = mm(load(invs[3]), load(links[0]))
    store(matrix_at(qt, 0), middle)
    raised = tuple(pltpu.roll(x, ROWS - 1, 2) for x in load(invs[0]))
    whole = mm(raised, middle)
    store(matrix_at(qx, 2), tuple(jnp.where(t_of == ROWS - 1, b, a) for a, b in zip(whole, middle)))

    for nu in (1, 2):
        middle = mm(load(invs[3]), load(links[nu]))
        store(matrix_at(middles, 1 + nu), middle)
        store(matrix_at(qt, nu), mm(middle, m_shift(load(links[3]), nu, 1)))

    store(slab, time_scan(load(links[3]), True))


    pl.semaphore_wait(barrier, len(partners))

    got_ux, got_qx = {}, {}

    def send_x(nu):
        got_ux[nu] = send(links[nu], matrix_at(ahead_x, nu - 1), x_down)
        got_qx[nu] = send(matrix_at(qx, nu - 1), matrix_at(qx_in, nu - 1), x_up)

    send_x(3)
    send_x(1)
    got_ut = send(inv.at[0 : 3 * MAT, 0:1, :], row_of(ahead_t, 0), t_down)
    got_qt = send(row_of(qt, 7), row_of(qt_in, 7), t_up)
    slab_copies = []
    far_order = sorted(range(1, n_ta), key=lambda d: -min(d, n_ta - d))
    for d in far_order:
        at = d - 1
        row = at // 2
        copy = pltpu.make_async_remote_copy(
            src_ref=row_of(slab, 0),
            dst_ref=row_of(matrix_at(slabs, at % 2), row),
            send_sem=slab_send.at[at],
            recv_sem=slab_recv.at[at],
            device_id=(around[at], j),
            device_id_type=MESH,
        )
        copy.start()
        slab_copies.append(copy)
    got_inv_xt = send(row_of(invs[0], 0), row_of(ahead_xt, 0), x_up_t_down)
    got_u_xt = send(row_of(links[3], 7), row_of(behind_xt, 7), x_down_t_up)


    scan = time_scan(load(links[3]), False)
    store(prefix, unit_where(tuple(pltpu.roll(x, 1, 2) for x in scan), t_of == 0))

    u_1, u_2 = load(links[1]), load(links[2])
    n_12 = mm(m_shift(u_2, 1, 1), m_shift(load(invs[1]), 2, 1))
    m_12 = mm(load(invs[2]), u_1)
    a_12 = less_inverse(mm(u_1, mm(n_12, load(invs[2]))))
    store(matrix_at(acc, 1), sub(a_12, m_shift(less_inverse(mm(m_12, n_12)), 2, -1)))
    store(matrix_at(acc, 2), sub(m_shift(less_inverse(mm(n_12, m_12)), 1, -1), a_12))

    send_x(2)

    got_ut.wait_recv()

    def inv_ahead(nu):
        return load_row(matrix_at(ahead_t, nu), 0)

    got_qt.wait_recv()

    def behind_t(nu):
        return load_row(matrix_at(qt_in, nu), 7)

    for nu in (1, 2):
        n_nt = mm(m_shift(load(links[3]), nu, 1), m_shift(load(invs[nu]), 3, 1, inv_ahead(nu)))
        a_nt = less_inverse(mm(load(links[nu]), mm(n_nt, load(invs[3]))))
        m_nt = load(matrix_at(middles, 1 + nu))
        lower = mm(m_shift(load(matrix_at(qt, nu)), 3, -1, behind_t(nu)), load(invs[nu]))
        accumulate(nu, sub(a_nt, less_inverse(lower)), 1)
        to_t = sub(m_shift(less_inverse(mm(n_nt, m_nt)), nu, -1), a_nt)
        if nu == 1:
            store(matrix_at(acc, 3), to_t)
        else:
            accumulate(3, to_t, 1)

    for copy in slab_copies:
        copy.wait_recv()
    slot = 2 * t_of
    even, odd = load(matrix_at(slabs, 0)), load(matrix_at(slabs, 1))
    if n_ta - 1 < 2 * ROWS - 1:
        even = unit_where(even, slot >= n_ta - 1)
    odd = unit_where(odd, slot + 1 >= n_ta - 1)
    others = mm(even, odd)
    for step in (1, 2, 4):
        others = mm(others, tuple(pltpu.roll(x, ROWS - step, 2) for x in others))
    others = tuple(jnp.broadcast_to(x[:, :, 0:1, :], x.shape) for x in others)
    line = mm(mm(load(slab), others), load(prefix))
    back = adj(line)
    former = (add_diagonal(FUGACITY * line[0], 1.0), FUGACITY * line[1])
    latter = (add_diagonal(ANTI_FUGACITY * back[0], 1.0), ANTI_FUGACITY * back[1])
    drift = sub(inverse(latter), inverse(former))
    weight = 4.0 * 3.0 / COUPLING
    accumulate(3, (weight * drift[0], weight * drift[1]), 1)

    def x_plane(nu):
        got_ux[nu].wait_recv()
        halo = inv_ahead(0) if nu == 3 else (None, None)
        n_xn = mm(load(matrix_at(ahead_x, nu - 1)), m_shift(load(invs[0]), nu, 1, halo))
        a_xn = less_inverse(mm(load(links[0]), mm(n_xn, load(invs[nu]))))
        if nu == 3:
            got_u_xt.wait_recv()
            ahead = load_row(behind_xt, 7)
            corner = mm(load(matrix_at(qt, 0)), load(matrix_at(ahead_x, 2)))
            corner = m_shift(corner, 3, -1, mm(behind_t(0), ahead))
            store(matrix_at(acc, 0), sub(a_xn, less_inverse(mm(corner, load(invs[0])))))
        else:
            m_xn = load(matrix_at(middles, nu - 1))
            lower = m_shift(less_inverse(mm(m_xn, n_xn)), nu, -1)
            accumulate(0, sub(a_xn, lower), 1)
        got_qx[nu].wait_recv()
        corner = load(matrix_at(qx_in, nu - 1))
        if nu == 3:
            got_inv_xt.wait_recv()
            ahead = load_row(ahead_xt, 0)
            fixed = mm(ahead, corner)
            corner = tuple(jnp.where(t_of == ROWS - 1, b, a) for a, b in zip(corner, fixed))
        accumulate(nu, sub(less_inverse(mm(load(links[nu]), corner)), a_xn), 1)

    x_plane(3)
    x_plane(1)

    loads[4].wait()
    c = math.sqrt(STEP_SIZE)

    def update(d):
        x = load(matrix_at(acc, d))
        w = -STEP_SIZE * COUPLING / 3.0
        mean_r = (x[0][0, 0] + x[0][1, 1] + x[0][2, 2]) * (1.0 / 3.0)
        mean_i = (x[1][0, 0] + x[1][1, 1] + x[1][2, 2]) * (1.0 / 3.0)
        n = [c * noise[d, a] for a in range(8)]
        n7 = n[7] * (1.0 / math.sqrt(3.0))
        real = {(0, 1): n[1], (0, 2): n[4], (1, 2): n[6]}
        imag = {(0, 1): n[0], (0, 2): n[3], (1, 2): n[5]}
        diag = (n[2] + n7, n7 - n[2], -2.0 * n7)
        yr, yi = [], []
        for a in range(3):
            row_r, row_i = [], []
            for b in range(3):
                if a == b:
                    row_r.append(w * (x[0][a, b] - mean_r))
                    row_i.append(w * (x[1][a, b] - mean_i) + diag[a])
                elif a < b:
                    row_r.append(w * x[0][a, b] + real[a, b])
                    row_i.append(w * x[1][a, b] + imag[a, b])
                else:
                    row_r.append(w * x[0][a, b] - real[b, a])
                    row_i.append(w * x[1][a, b] + imag[b, a])
            yr.append(jnp.stack(row_r))
            yi.append(jnp.stack(row_i))
        return exp_times((jnp.stack(yr), jnp.stack(yi)), load(links[d]))


    def exchange(step, link, order):
        plus = minus = None
        got = {}
        for d in order:
            m = link(d)
            rows, columns = gram_rows(m), h_pack(gram_cols(m))
            plus = rows if plus is None else h_add(plus, rows)
            if d == 0:
                mine = herm_at(gx, step)
                mine[...] = columns
                got["x"] = send(mine, herm_at(gx_in, step), x_up)
                there = row_of(herm_at(gx_in, 2 + step), 0)
                got["x ahead"] = send(row_of(mine, 0), there, x_up_t_down)
                continue
            if d == 3:
                mine = herm_at(gt, step)
                mine[...] = columns
                mine = row_of(mine, 7)
                got["t"] = send(mine, row_of(herm_at(gt_in, step), 7), t_up)
                got["t ahead"] = send(mine, row_of(herm_at(gt_in, 2 + step), 7), x_down_t_up)
                lagged = jnp.where(index_of(0, 3) == 0, 0.0, pltpu.roll(columns, 1, 1))
            else:
                lagged = shift(columns, d, -1)
            minus = lagged if minus is None else minus + lagged
        mine = herm_at(part, step)
        mine[...] = h_pack(plus) - minus
        got["part x"] = send(mine, herm_at(part_in, step), x_down)
        got["part t"] = send(row_of(mine, 0), row_of(herm_at(part_in, 2 + step), 0), t_down)
        return plus[0][0] + plus[0][1] + plus[0][2], got

    def transforms(step, got):
        first = index_of(0, 3) == 0
        got["t"].wait_recv()
        got["x"].wait_recv()
        lag = jnp.where(first, herm_at(gt_in, step)[:, 7:8, :], 0.0)
        here = herm_at(part, step)[...] - herm_at(gx_in, step)[...] - lag
        low, high = cooling_pair(h_unpack(here))

        def ahead(d):
            if d == 3:
                got["part t"].wait_recv()
                got["x ahead"].wait_recv()
                g = herm_at(part_in, 2 + step)[:, 0:1, :] - herm_at(gx_in, 2 + step)[:, 0:1, :]
                g = g - herm_at(gt, step)[:, 7:8, :]
                halo = h_pack(cooling_pair(h_unpack(g))[1])
                return h_unpack(shift(h_pack(high), 3, 1, halo))
            if d == 0:
                got["t ahead"].wait_recv()
                got["part x"].wait_recv()
                g = herm_at(part_in, step)[...] - herm_at(gx, step)[...]
                g = g - jnp.where(first, herm_at(gt_in, 2 + step)[:, 7:8, :], 0.0)
                return cooling_pair(h_unpack(g))[1]
            return h_shift(high, d, 1)

        return low, ahead

    def lane_sums(value):
        return jnp.sum(value, axis=1, keepdims=True)

    def first_links(d):
        if d == 0:
            x_plane(2)
        m = update(d)
        store(matrix_at(new, d), m)
        return m

    norm, got = exchange(0, first_links, (3, 1, 0, 2))
    norms = [lane_sums(norm)]
    low, ahead = transforms(0, got)

    def cooled_link(d):
        m = h_times(low, load(matrix_at(new, d)))
        return times_h(m, ahead(d))

    def second_links(d):
        m = cooled_link(d)
        store(matrix_at(new, d), m)
        return m

    norm, got = exchange(1, second_links, (1, 2, 3, 0))
    norms.append(lane_sums(norm))
    low, ahead = transforms(1, got)

    total = None
    for d in (1, 2, 3, 0):
        m = cooled_link(d)
        store(matrix_at(out, d), m)
        squares = m[0] * m[0] + m[1] * m[1]
        squares = squares[0] + squares[1] + squares[2]
        squares = squares[0] + squares[1] + squares[2]
        total = squares if total is None else total + squares
    norms.append(lane_sums(total))


    row, lane = index_of(0, 2), index_of(1, 2)
    spread = jnp.zeros(TILE, jnp.float32)
    for at, sums in enumerate(norms):
        spread = jnp.where(lane == row + ROWS * at, sums, spread)
    mine = jnp.sum(spread, axis=0, keepdims=True)
    norm_row[0:1, :] = mine
    norm_rows[j, 0:1, :] = mine

    def norm_copy(d, at):
        return pltpu.make_async_remote_copy(
            src_ref=norm_row.at[0:1, :],
            dst_ref=norm_rows.at[at, 0:1, :],
            send_sem=norm_send.at[d],
            recv_sem=norm_recv.at[at],
            device_id=(k, group[d]),
            device_id_type=MESH,
        )

    norm_copies = [norm_copy(d, j) for d in range(n_sa - 1)]
    for copy in norm_copies:
        copy.start()
    for copy in started + slab_copies:
        copy.wait_send()
    for d in range(n_sa - 1):
        norm_copy(d, group[d]).wait_recv()
    total = norm_rows[0, 0:1, :]
    for at in range(1, n_sa):
        total = total + norm_rows[at, 0:1, :]
    total = total * (1.0 / (4.0 * n_sa * LANES)) - 3.0
    for at in range(3):
        norm_ref[at : at + 1, :] = total[:, ROWS * at : ROWS * (at + 1)]
    for copy in norm_copies:
        copy.wait_send()


def finish(links, norms, links_out, norms_out, sem):
    copies = (
        pltpu.make_async_copy(links, links_out, sem.at[0]),
        pltpu.make_async_copy(norms, norms_out, sem.at[1]),
    )
    for copy in copies:
        copy.start()
    for copy in copies:
        copy.wait()


def local(gauge_links, noise_field):
    n_ta, n_sa = lax.axis_size("ta"), lax.axis_size("sa")
    n_in = max(n_sa // 4, 2)
    shape = (4 * MAT,) + TILE
    vmem = lambda *s: pltpu.VMEM(s, jnp.float32)
    dma = lambda n: pltpu.SemaphoreType.DMA((n,))
    cooled, norms = pl.pallas_call(
        functools.partial(kernel, (n_ta, n_sa, n_in)),
        out_shape=(
            pltpu.VMEM(shape, jnp.float32),
            pltpu.VMEM((3, ROWS), jnp.float32),
        ),
        in_specs=[pl.BlockSpec(memory_space=pltpu.HBM)] * 2,
        out_specs=(pl.BlockSpec(memory_space=pltpu.VMEM),) * 2,
        scratch_shapes=[
            vmem(*shape),
            vmem(4, 8, *TILE),
            vmem(*shape),
            vmem(3 * MAT, *TILE),
            vmem(3 * MAT, *TILE),
            vmem(MAT, *TILE),
            vmem(MAT, *TILE),
            vmem(3 * MAT, *TILE),
            vmem(3 * MAT, *TILE),
            vmem(3 * MAT, *TILE),
            vmem(3 * MAT, *TILE),
            vmem(MAT, *TILE),
            vmem(2 * MAT, *TILE),
            vmem(MAT, *TILE),
            vmem(4 * MAT, *TILE),
            vmem(*shape),
            vmem(*shape),
            vmem(2 * HERM, *TILE),
            vmem(4 * HERM, *TILE),
            vmem(2 * HERM, *TILE),
            vmem(4 * HERM, *TILE),
            vmem(2 * HERM, *TILE),
            vmem(4 * HERM, *TILE),
            vmem(*TILE),
            vmem(n_sa, *TILE),
            dma(5),
            dma(22),
            dma(22),
            dma(n_ta - 1),
            dma(n_ta - 1),
            dma(n_sa - 1),
            dma(n_sa),
        ],
        compiler_params=pltpu.CompilerParams(
            collective_id=0, has_side_effects=True, vmem_limit_bytes=VMEM_LIMIT
        ),
        name="langevin_step",
    )(
        pltpu.with_memory_space_constraint(gauge_links.reshape(shape), pltpu.HBM),
        pltpu.with_memory_space_constraint(noise_field.reshape((4, 8) + TILE), pltpu.HBM),
    )
    cooled, norms = pl.pallas_call(
        finish,
        out_shape=(
            jax.ShapeDtypeStruct(shape, jnp.float32),
            jax.ShapeDtypeStruct((3, ROWS), jnp.float32),
        ),
        in_specs=[pl.BlockSpec(memory_space=pltpu.VMEM)] * 2,
        out_specs=(pl.BlockSpec(memory_space=pltpu.HBM),) * 2,
        scratch_shapes=[dma(2)],
        compiler_params=pltpu.CompilerParams(vmem_limit_bytes=VMEM_LIMIT),
        name="write_out",
    )(cooled, norms)
    return cooled.reshape(gauge_links.shape), norms


def solution(mesh):
    placed = (P(None, None, None, None, "sa", "ta", None), P(None, None, "sa", "ta", None))
    return jax.shard_map(
        local,
        mesh=mesh,
        in_specs=placed,
        out_specs=(P(None, None, None, None, "sa", "ta", None), P(None, "ta")),
        check_vma=False,
    )
```
